256 devices in a mesh: ctx: 8 (over x_hi, y), dp: 32 (over z, x_lo, core).
Axes of the slice: x: 4 (x_hi: 2, x_lo: 2; x = x_hi * 2 + x_lo), y: 4, z: 8, core: 2. Of those that a mesh axis runs over, the one named last changes fastest.
Arguments:
- query_gate: bfloat16 [32, 1024, 4096], P('dp', 'ctx'), may hold values from -0.3125 to 0.3125
- key_gate: bfloat16 [32, 1024, 4096], P('dp', 'ctx'), may hold values from -6 to 6
- value_in: bfloat16 [32, 1024, 4096], P('dp', 'ctx'), may hold values from -6 to 6
- conv_out: bfloat16 [32, 1024, 4096], P('dp', 'ctx'), may hold values from -6 to 6
- out_grad: bfloat16 [32, 1024, 4096], P('dp', 'ctx'), may hold values from -6 to 6
- filters: float32 [2048, 1024], P('dp', 'ctx'), may hold values from -8 to 8
Outputs:
- query_grad: bfloat16 [32, 1024, 4096], P('dp', 'ctx')
- key_grad: bfloat16 [32, 1024, 4096], P('dp', 'ctx')
- value_grad: bfloat16 [32, 1024, 4096], P('dp', 'ctx')
- filter_grad: float32 [2048, 1024], P('dp', 'ctx')
The draws below stay inside these ranges and needn't reach their ends.
All inputs are finite; a program needn't handle non-finite values.
Results may differ from the reference program's by a relative error of at most 0.013.
Values may be sent and summed in bfloat16 or wider, within the bound.
No kernel may reach another device: no remote copies, remote signals or barrier semaphores. Data moves between devices by JAX's collectives and lax.ppermute only.
A program may use at most 320 MiB of HBM per device.

```python
import jax
import jax.numpy as jnp
from jax import lax

D = 4096
DH = 2048
SEQ = 1024
NSEQ = 32


def shard_levels(key, dims, cuts, low, top_value):
    def one(position, parts):
        draws = jax.random.uniform(jax.random.fold_in(jax.random.fold_in(key, 6), position), (parts,), jnp.float32, low / len(cuts), top_value / len(cuts))
        return jnp.repeat(jnp.exp(draws), dims[position] // parts).reshape((-1,) + (1,) * (len(dims) - position - 1))

    factor_of = one(*cuts[0])
    for cut in cuts[1:]:
        factor_of = factor_of * one(*cut)
    return factor_of


def bell_draw(key, dims, scale, bound, pieces=(), dtype=jnp.bfloat16):
    array = jax.random.normal(key, dims, jnp.float32) * scale
    if len(pieces) > 0:
        array = shard_levels(key, dims, pieces, -0.22, 0.18) * array
    return jnp.clip(array, min=-bound, max=bound).astype(dtype)


def setup_inputs(seed: int = 0) -> dict:
    streams_of = jax.random.split(jax.random.key(seed), 7)
    query_gate = bell_draw(streams_of[0], (NSEQ, SEQ, D), (4.0 / (NSEQ * SEQ) ** 0.5), 0.3125, ((0, 32), (1, 8)))
    key_gate = bell_draw(streams_of[1], (NSEQ, SEQ, D), 1.0, 6.0, ((0, 32), (1, 8)))
    value_in = bell_draw(streams_of[2], (NSEQ, SEQ, D), 1.0, 6.0, ((0, 32), (1, 8)))
    conv_out = bell_draw(streams_of[3], (NSEQ, SEQ, D), 1.0, 6.0, ((0, 32), (1, 8)))
    out_grad = bell_draw(streams_of[4], (NSEQ, SEQ, D), 1.0, 6.0, ((0, 32), (1, 8)))
    filters = bell_draw(streams_of[5], (DH, SEQ), 2.0, 8.0, ((0, 32), (1, 8)), jnp.float32)
    return {"query_gate": query_gate, "key_gate": key_gate, "value_in": value_in, "conv_out": conv_out, "out_grad": out_grad, "filters": filters}


def reference(query_gate, key_gate, value_in, conv_out, out_grad, filters):
    length = query_gate.shape[1]
    half_width = query_gate.shape[2] // 2
    filter_spec = jnp.fft.rfft(filters.T, n=2 * length, axis=0)

    def one_sequence(carry, items):
        query_row, key_row, value_row, conv_row, grad_row = items
        key_float = key_row.astype(jnp.float32)
        value_float = value_row.astype(jnp.float32)
        grad_float = grad_row.astype(jnp.float32)
        mixed = (key_float * value_float).astype(jnp.bfloat16)
        grad_mix = (grad_float * query_row.astype(jnp.float32)).astype(jnp.bfloat16)
        mixed, grad_mix = lax.optimization_barrier((mixed, grad_mix))
        mixed_cols = jnp.stack([mixed[:, :half_width], mixed[::-1, half_width:][:, ::-1]], axis=1).astype(jnp.float32)
        grad_cols = jnp.stack([grad_mix[:, :half_width], grad_mix[::-1, half_width:][:, ::-1]], axis=1).astype(jnp.float32)
        mixed_spec = jnp.fft.rfft(mixed_cols, n=2 * length, axis=0)
        grad_spec = jnp.fft.rfft(grad_cols, n=2 * length, axis=0)
        conv_cols = jnp.fft.irfft(grad_spec * jnp.conj(filter_spec)[:, None, :], n=2 * length, axis=0)[:length]
        lag_cols = jnp.fft.irfft(grad_spec * jnp.conj(mixed_spec), n=2 * length, axis=0)[:length]
        conv_grad = jnp.concatenate([conv_cols[:, 0], conv_cols[::-1, 1][:, ::-1]], axis=1).astype(jnp.bfloat16)
        conv_grad = lax.optimization_barrier(conv_grad)
        conv_float = conv_grad.astype(jnp.float32)
        query_grad = (grad_float * conv_row.astype(jnp.float32)).astype(jnp.bfloat16)
        key_grad = (conv_float * value_float).astype(jnp.bfloat16)
        value_grad = (conv_float * key_float).astype(jnp.bfloat16)
        lag_sum = jnp.sum(lag_cols, axis=1).T.astype(jnp.float32)
        return carry + lag_sum, (query_grad, key_grad, value_grad)

    start_grad = jnp.zeros((half_width, length), jnp.float32)
    filter_grad, outputs = lax.scan(one_sequence, start_grad, (query_gate, key_gate, value_in, conv_out, out_grad))
    return outputs[0], outputs[1], outputs[2], filter_grad
```

```python
import functools

import jax
import jax.numpy as jnp
import numpy as np
from jax import lax
from jax.experimental import pallas as pl
from jax.experimental.pallas import tpu as pltpu
from jax.sharding import Mesh
from jax.sharding import PartitionSpec as P

CTX = ("xh", "y")
PLANE = ("xh", "y", "xl", "core")
CTX_Z = ("xh", "y", "z")
SEQ = 1024
BLOCK = 128
LANES = 128
SPLIT = 4
FREQ = 128
MIB = 1024 * 1024
F32 = jnp.float32
BF16 = jnp.bfloat16


def half_tables():
    odd = 2 * np.arange(SEQ, dtype=np.int64) + 1
    phase = np.multiply.outer(odd, odd) % (8 * SEQ)
    angle = phase.astype(np.float64) * (np.pi / (4 * SEQ))
    return np.cos(angle), np.sin(angle)


def half_turn():
    angle = np.pi * (2 * np.arange(SEQ) + 1) / (4 * SEQ)
    return np.cos(angle), np.sin(angle)


def dot(a, b):
    return jnp.dot(a, b, preferred_element_type=F32)


def dot_nt(a, b):
    return lax.dot_general(a, b, (((1,), (1,)), ((), ())), preferred_element_type=F32)


def dot_tn(a, b):
    return lax.dot_general(a, b, (((0,), (0,)), ((), ())), preferred_element_type=F32)


def pack_kernel(*refs):
    out_ref = refs[8]
    tiles = refs[0].shape[1] // LANES
    low = lax.broadcasted_iota(jnp.int32, (BLOCK, LANES), 1) < LANES // 2
    for t in range(tiles):
        ahead = pl.ds(t * LANES, LANES)
        behind = pl.ds((tiles - 1 - t) * LANES, LANES)
        for kind in range(2):
            a, b = refs[2 * kind], refs[2 * kind + 1]
            c, d = refs[4 + 2 * kind], refs[5 + 2 * kind]
            f = a[:, ahead].astype(F32) * b[:, ahead].astype(F32)
            r = c[:, behind].astype(F32) * d[:, behind].astype(F32)
            out_ref[2 * t, kind] = jnp.where(low, f, r).astype(BF16)
            out_ref[2 * t + 1, kind] = jnp.where(low, r, f).astype(BF16)


def pack(q, g, k, v):
    steps = 4
    width = q.shape[1] // (2 * steps)
    ahead = pl.BlockSpec((BLOCK, width), lambda j: (0, j))
    behind = pl.BlockSpec((BLOCK, width), lambda j: (0, 2 * steps - 1 - j))
    return pl.pallas_call(
        pack_kernel,
        grid=(steps,),
        in_specs=[ahead] * 4 + [behind] * 4,
        out_specs=pl.BlockSpec((8, 2, BLOCK, LANES), lambda j: (j, 0, 0, 0)),
        out_shape=jax.ShapeDtypeStruct((32, 2, BLOCK, LANES), BF16),
        compiler_params=pltpu.CompilerParams(vmem_limit_bytes=16 * MIB),
        cost_estimate=pl.CostEstimate(flops=2 * MIB, bytes_accessed=6 * MIB, transcendentals=0),
        name="pack",
    )(q, g, k, v, q, g, k, v)


def filter_kernel(rows_ref, cos_ref, sin_ref, turn_cos_ref, turn_sin_ref, sign_ref, out_ref):
    rows = rows_ref[...]
    fc = dot_nt(cos_ref[...], rows)
    fs = dot_nt(sin_ref[...], rows)
    tc, ts = turn_cos_ref[...], turn_sin_ref[...]
    out_ref[0] = fc * tc + fs * ts
    out_ref[1] = (fc * ts - fs * tc) * sign_ref[...]


def filter_spectrum(rows, cos, sin, turn_cos, turn_sin, sign):
    return pl.pallas_call(
        filter_kernel,
        out_shape=jax.ShapeDtypeStruct((2, SEQ, LANES), F32),
        compiler_params=pltpu.CompilerParams(vmem_limit_bytes=24 * MIB),
        cost_estimate=pl.CostEstimate(flops=512 * MIB, bytes_accessed=5 * MIB, transcendentals=0),
        name="filter_spectrum",
    )(rows, cos, sin, turn_cos, turn_sin, sign)


def spectrum_kernel(x_ref, cos_ref, sin_ref, filt_ref, turn_cos_ref, turn_sin_ref, sign_ref, fold_ref,
                    uv_ref, fg_ref, cols, prod):
    width = SPLIT * LANES
    for i in range(SEQ // BLOCK):
        for q in range(SPLIT):
            for kind in range(2):
                cols[pl.ds(i * BLOCK, BLOCK), pl.ds(kind * width + q * LANES, LANES)] = x_ref[SPLIT * i + q, kind]
    sign = sign_ref[...]

    def step(n, _):
        at = pl.multiple_of(n * FREQ, FREQ)
        rows = pl.ds(at, FREQ)
        values = cols[...]
        c = dot(cos_ref[rows, :], values)
        s = dot(sin_ref[rows, :], values)
        re, im = filt_ref[0, rows, :], filt_ref[1, rows, :]
        sum_re = sum_im = None
        for q in range(SPLIT):
            lanes = slice(q * LANES, (q + 1) * LANES)
            other = slice(width + q * LANES, width + (q + 1) * LANES)
            cg, sg, cm, sm = c[:, lanes], s[:, lanes], c[:, other], s[:, other]
            uv_ref[rows, lanes] = (cg * re + sg * im).astype(BF16)
            uv_ref[pl.ds(pl.multiple_of(SEQ + at, FREQ), FREQ), lanes] = (sg * re - cg * im).astype(BF16)
            a, b = cg * cm + sg * sm, cg * sm - sg * cm
            sum_re = a if sum_re is None else sum_re + a
            sum_im = b if sum_im is None else sum_im + b
        sum_im = -sum_im * sign
        tc, ts = turn_cos_ref[rows, :], turn_sin_ref[rows, :]
        prod[rows, :] = (sum_re * tc + sum_im * ts).astype(BF16)
        prod[pl.ds(pl.multiple_of(SEQ + at, FREQ), FREQ), :] = (sum_re * ts - sum_im * tc).astype(BF16)
        return 0

    lax.fori_loop(0, SEQ // FREQ, step, 0)
    lags = dot_tn(prod[:SEQ, :], cos_ref[...]) + dot_tn(prod[SEQ:, :], sin_ref[...])
    fg_ref[...] = jnp.dot(fold_ref[...], lags * (1.0 / SEQ), precision=lax.Precision.HIGHEST,
                          preferred_element_type=F32)


def spectra(x, cos, sin, filt, turn_cos, turn_sin, sign, fold):
    return pl.pallas_call(
        spectrum_kernel,
        out_shape=(
            jax.ShapeDtypeStruct((2 * SEQ, SPLIT * LANES), BF16),
            jax.ShapeDtypeStruct((LANES // 2, SEQ), F32),
        ),
        scratch_shapes=[
            pltpu.VMEM((SEQ, 2 * SPLIT * LANES), BF16),
            pltpu.VMEM((2 * SEQ, LANES), BF16),
        ],
        compiler_params=pltpu.CompilerParams(vmem_limit_bytes=40 * MIB),
        cost_estimate=pl.CostEstimate(flops=4300 * MIB, bytes_accessed=9 * MIB, transcendentals=0),
        name="spectra",
    )(x, cos, sin, filt, turn_cos, turn_sin, sign, fold)


def back_kernel(uv_ref, cos_ref, sin_ref, out_ref):
    for i in range(SEQ // BLOCK):
        rows = pl.ds(i * BLOCK, BLOCK)
        conv = dot(cos_ref[rows, :], uv_ref[:SEQ, :]) + dot(sin_ref[rows, :], uv_ref[SEQ:, :])
        conv = (conv * (1.0 / SEQ)).astype(BF16)
        for q in range(SPLIT):
            out_ref[SPLIT * i + q] = conv[:, q * LANES:(q + 1) * LANES]


def back(uv, cos, sin):
    return pl.pallas_call(
        back_kernel,
        out_shape=jax.ShapeDtypeStruct((32, BLOCK, LANES), BF16),
        compiler_params=pltpu.CompilerParams(vmem_limit_bytes=32 * MIB),
        cost_estimate=pl.CostEstimate(flops=2100 * MIB, bytes_accessed=7 * MIB, transcendentals=0),
        name="back",
    )(uv, cos, sin)


def unpack_kernel(conv_ref, ka_ref, va_ref, kb_ref, vb_ref, key_ref, value_ref):
    tiles = ka_ref.shape[1] // LANES
    low = lax.broadcasted_iota(jnp.int32, (BLOCK, LANES), 1) < LANES // 2
    strand = pl.program_id(1)

    def run(k_ref, v_ref, ahead):
        for t in range(tiles):
            even, odd = conv_ref[2 * t].astype(F32), conv_ref[2 * t + 1].astype(F32)
            at = t if ahead else tiles - 1 - t
            lanes = pl.ds(at * LANES, LANES)
            conv = jnp.where(low, even, odd) if ahead else jnp.where(low, odd, even)
            key_ref[:, lanes] = (conv * v_ref[:, lanes].astype(F32)).astype(BF16)
            value_ref[:, lanes] = (conv * k_ref[:, lanes].astype(F32)).astype(BF16)

    @pl.when(strand == 0)
    def _():
        run(ka_ref, va_ref, True)

    @pl.when(strand == 1)
    def _():
        run(kb_ref, vb_ref, False)


def unpack(conv, k, v):
    steps = 4
    width = k.shape[1] // (2 * steps)
    ahead = pl.BlockSpec((BLOCK, width), lambda j, s: (0, j))
    behind = pl.BlockSpec((BLOCK, width), lambda j, s: (0, 2 * steps - 1 - j))
    either = pl.BlockSpec((BLOCK, width), lambda j, s: (0, jnp.where(s == 0, j, 2 * steps - 1 - j)))
    shape = jax.ShapeDtypeStruct(k.shape, BF16)
    return pl.pallas_call(
        unpack_kernel,
        grid=(steps, 2),
        in_specs=[pl.BlockSpec((8, BLOCK, LANES), lambda j, s: (j, 0, 0)), ahead, ahead, behind, behind],
        out_specs=(either, either),
        out_shape=(shape, shape),
        compiler_params=pltpu.CompilerParams(vmem_limit_bytes=16 * MIB),
        cost_estimate=pl.CostEstimate(flops=2 * MIB, bytes_accessed=5 * MIB, transcendentals=0),
        name="unpack",
    )(conv, k, v, k, v)


def swap_z(block, bit):
    return lax.ppermute(block, "z", [(i, i ^ (1 << bit)) for i in range(8)])


def turned(block, flip):
    route = [(8 * l + a, 8 * a + l) for l in range(8) for a in range(8)]
    if flip:
        route = [(8 * a + l, 8 * (l ^ 1) + a) for l in range(8) for a in range(8)]
    return lax.ppermute(block, CTX_Z, route)


def gathered_lags(filters):
    block = turned(filters.astype(BF16), False)
    z = lax.axis_index("z")
    for bit in range(3):
        other = swap_z(block, bit)
        first = (z >> bit) % 2 == 0
        block = jnp.concatenate([jnp.where(first, block, other), jnp.where(first, other, block)], axis=1)
    return block


def reduced_lags(partial):
    z = lax.axis_index("z")
    for bit in (2, 1):
        half = partial.shape[1] // 2
        low, high = partial[:, :half], partial[:, half:]
        first = (z >> bit) % 2 == 0
        kept, given = jnp.where(first, low, high), jnp.where(first, high, low)
        partial = kept + swap_z(given, bit)
    first = z % 2 == 0
    low, high = partial[:, :BLOCK], partial[:, BLOCK:]
    own, other = jnp.where(first, low, high), jnp.where(first, high, low)
    return turned(own, False) + turned(other, True)


def local(query_gate, key_gate, value_in, conv_out, out_grad, filters):
    cos64, sin64 = half_tables()
    cos, sin = jnp.asarray(cos64, BF16), jnp.asarray(sin64, BF16)
    turn_cos, turn_sin = (jnp.asarray(np.tile(t[:, None], (1, LANES)), F32) for t in half_turn())
    odd = lax.axis_index("core") == 1
    lane = np.arange(LANES)
    sign = np.where(lane < LANES // 2, -1.0, 1.0).astype(np.float32)[None]
    sign = jnp.where(odd, -sign, sign)
    row = np.arange(LANES // 2)[:, None]
    fold_even = ((lane == row) | (lane == LANES - 1 - row)).astype(np.float32)
    fold = jnp.where(odd, fold_even[::-1], fold_even)

    q, k, v, g = query_gate[0], key_gate[0], value_in[0], out_grad[0]
    x = pack(q, g, k, v)
    x = lax.all_to_all(x, PLANE, split_axis=0, concat_axis=0, tiled=True)

    query_grad = (out_grad.astype(F32) * conv_out.astype(F32)).astype(BF16)
    lags = gathered_lags(filters)
    mirrored = lags[::-1]
    rows = jnp.concatenate([jnp.where(odd, mirrored, lags), jnp.where(odd, lags, mirrored)], axis=0)
    filt = filter_spectrum(rows, cos, sin, turn_cos, turn_sin, sign)

    uv, partial = spectra(x, cos, sin, filt, turn_cos, turn_sin, sign, fold)
    conv = back(uv, cos, sin)
    conv = lax.all_to_all(conv, PLANE, split_axis=0, concat_axis=0, tiled=True)
    filter_grad = reduced_lags(partial)
    key_grad, value_grad = unpack(conv, k, v)
    return query_grad, key_grad[None], value_grad[None], filter_grad


def solution(mesh):
    fine = Mesh(mesh.devices.reshape(2, 4, 8, 2, 2), ("xh", "y", "z", "xl", "core"))
    wide = P(("z", "xl", "core"), CTX, None)
    narrow = P(("z", "xl", "core"), CTX)
    return jax.shard_map(
        local,
        mesh=fine,
        in_specs=(wide,) * 5 + (narrow,),
        out_specs=(wide, wide, wide, narrow),
        check_vma=False,
    )
```

```python
import functools

import jax
import jax.numpy as jnp
import numpy as np
from jax import lax
from jax.experimental import pallas as pl
from jax.experimental.pallas import tpu as pltpu
from jax.sharding import Mesh
from jax.sharding import PartitionSpec as P

CTX = ("xh", "y")
PLANE = ("xh", "y", "xl", "core")
CTX_Z = ("xh", "y", "z")
SEQ = 1024
BLOCK = 128
LANES = 128
SPLIT = 4
WIDTH = SPLIT * LANES
GROUPS = 32
STEP = 32
CUTS = 4
MIB = 1024 * 1024
F32 = jnp.float32
BF16 = jnp.bfloat16
OWNER = (3, 0, 2, 1, 5, 6, 4, 7)
LAG_AT = (5, 7, 6, 4, 2, 0, 1, 3)


def chunk_of(block):
    return 4 * OWNER[block // 4] + block % 4


def slot_of(z, lag_block):
    n = z ^ LAG_AT[lag_block]
    return (n & 1) * 4 + (n & 2) + (n >> 2)


def dot(a, b):
    return jnp.dot(a, b, preferred_element_type=F32)


def dot_nt(a, b):
    return lax.dot_general(a, b, (((1,), (1,)), ((), ())), preferred_element_type=F32)


def dot_tn(a, b):
    return lax.dot_general(a, b, (((0,), (0,)), ((), ())), preferred_element_type=F32)


def seeds():
    odd = 2 * np.arange(SEQ, dtype=np.int64) + 1
    coarse = 2 * STEP * np.arange(SEQ // STEP, dtype=np.int64)
    fine = 2 * np.arange(STEP, dtype=np.int64) + 1
    out = []
    for part in (coarse, fine):
        angle = (np.multiply.outer(part, odd) % (8 * SEQ)).astype(np.float64) * (np.pi / (4 * SEQ))
        out += [np.cos(angle), np.sin(angle)]
    return np.stack(out).astype(np.float32)


def fill_tables(seed, cos, sin, turn, first, last):
    for a in range(first // STEP, last // STEP):
        ca, sa = seed[0, a:a + 1, :], seed[1, a:a + 1, :]
        c = ca * seed[2] - sa * seed[3]
        s = sa * seed[2] + ca * seed[3]
        rows = pl.ds(a * STEP, STEP)
        cos[rows, :] = c.astype(BF16)
        sin[rows, :] = s.astype(BF16)
        turn[0, rows, :] = jnp.broadcast_to(c[:, :1], (STEP, LANES))
        turn[1, rows, :] = jnp.broadcast_to(s[:, :1], (STEP, LANES))


def lanes_of(tile):
    return slice(tile * LANES, (tile + 1) * LANES)


def pack_kernel(q_hbm, g_hbm, k_hbm, v_hbm, x_hbm, buf, out, sem_in, sem_out):
    tiles = GROUPS // 2 // CUTS
    width = tiles * LANES
    low = lax.broadcasted_iota(jnp.int32, (BLOCK, LANES), 1) < LANES // 2
    arriving = []
    for j in range(CUTS):
        copies = []
        for i, ref in enumerate((q_hbm, g_hbm, k_hbm, v_hbm)):
            for s, at in enumerate((j, 2 * CUTS - 1 - j)):
                cols = pl.ds(at * width, width)
                copies.append(pltpu.make_async_copy(ref.at[:, cols], buf.at[i, :, cols], sem_in.at[j, i, s]))
        for copy in copies:
            copy.start()
        arriving.append(copies)
    leaving = []
    for j in range(CUTS):
        for copy in arriving[j]:
            copy.wait()
        for t in range(j * tiles, (j + 1) * tiles):
            ahead, behind = lanes_of(t), lanes_of(GROUPS - 1 - t)
            even, odd = chunk_of(2 * t), chunk_of(2 * t + 1)
            for kind in range(2):
                a, b = 2 * kind, 2 * kind + 1
                f = buf[a, :, ahead].astype(F32) * buf[b, :, ahead].astype(F32)
                r = buf[a, :, behind].astype(F32) * buf[b, :, behind].astype(F32)
                out[even, kind] = jnp.where(low, f, r).astype(BF16)
                out[odd, kind] = jnp.where(low, r, f).astype(BF16)
            pair = pl.ds(even, 2)
            copy = pltpu.make_async_copy(out.at[pair], x_hbm.at[pair], sem_out.at[t])
            copy.start()
            leaving.append(copy)
    for copy in leaving:
        copy.wait()


ANY = pl.BlockSpec(memory_space=pl.ANY)
VMEM = pl.BlockSpec(memory_space=pltpu.VMEM)
SMEM = pl.BlockSpec(memory_space=pltpu.SMEM)
HBM = pl.BlockSpec(memory_space=pltpu.HBM)
LIMIT = pltpu.CompilerParams(vmem_limit_bytes=60 * MIB)
SMALL = pltpu.CompilerParams(vmem_limit_bytes=24 * MIB)


def pack(q, g, k, v):
    return pl.pallas_call(
        pack_kernel,
        in_specs=[ANY] * 4,
        out_specs=ANY,
        out_shape=jax.ShapeDtypeStruct((GROUPS, 2, BLOCK, LANES), BF16),
        scratch_shapes=[
            pltpu.VMEM((4,) + q.shape, BF16),
            pltpu.VMEM((GROUPS, 2, BLOCK, LANES), BF16),
            pltpu.SemaphoreType.DMA((CUTS, 4, 2)),
            pltpu.SemaphoreType.DMA((GROUPS // 2,)),
        ],
        compiler_params=LIMIT,
        cost_estimate=pl.CostEstimate(flops=2 * MIB, bytes_accessed=6 * MIB, transcendentals=0),
        name="pack",
    )(q, g, k, v)


def filter_kernel(place_ref, seed, near, far, filt, seed_out, rows_in, cos, sin, turn):
    odd, z = place_ref[0], place_ref[1]
    step = 256
    row = lax.broadcasted_iota(jnp.int32, (LANES, LANES // 2), 0)
    col = lax.broadcasted_iota(jnp.int32, (LANES, LANES // 2), 1)
    ahead = row - jnp.where(odd == 0, 0, LANES // 2)
    behind = jnp.where(odd == 0, LANES, LANES // 2) - 1 - row
    spread = jnp.where((col == ahead) | (col == behind), 1.0, 0.0).astype(BF16)
    for block in range(SEQ // BLOCK):
        slot = slot_of(z, block)
        lags = jnp.where(slot < 4, near[slot % 4], far[slot % 4])
        rows_in[:, lanes_of(block)] = dot(spread, lags).astype(BF16)
    sign = strand_sign(odd)
    for n in range(SEQ // step):
        fill_tables(seed, cos, sin, turn, n * step, (n + 1) * step)
        at = pl.ds(n * step, step)
        fc, fs = dot_nt(cos[at, :], rows_in[...]), dot_nt(sin[at, :], rows_in[...])
        tc, ts = turn[0, at, :], turn[1, at, :]
        filt[0, at, :] = fc * tc + fs * ts
        filt[1, at, :] = (fc * ts - fs * tc) * sign
    seed_out[...] = seed[...]


def filter_spectrum(place, near, far):
    seed = jnp.asarray(seeds())
    return pl.pallas_call(
        filter_kernel,
        in_specs=[SMEM, VMEM, VMEM, VMEM],
        out_specs=(VMEM, VMEM),
        out_shape=(
            jax.ShapeDtypeStruct((2, SEQ, LANES), F32),
            jax.ShapeDtypeStruct(seed.shape, F32),
        ),
        scratch_shapes=[
            pltpu.VMEM((LANES, SEQ), BF16),
            pltpu.VMEM((SEQ, SEQ), BF16),
            pltpu.VMEM((SEQ, SEQ), BF16),
            pltpu.VMEM((2, SEQ, LANES), F32),
        ],
        compiler_params=SMALL,
        cost_estimate=pl.CostEstimate(flops=1, bytes_accessed=1, transcendentals=0),
        name="filter_spectrum",
    )(place, seed, near, far)


def strand_sign(odd):
    lane = lax.broadcasted_iota(jnp.int32, (1, LANES), 1)
    return jnp.where((lane < LANES // 2) == (odd == 0), -1.0, 1.0).astype(F32)


def core_kernel(place_ref, x, filt, seed, conv_hbm, keep, give, cos, sin, turn, uv, prod, conv, folded, sem_out):
    odd, z = place_ref[0], place_ref[1]
    step = 256
    steps = SEQ // step
    sign = strand_sign(odd)
    def columns(kind):
        tiles = [[x[SPLIT * i + q, kind] for i in range(SEQ // BLOCK)] for q in range(SPLIT)]
        return jnp.concatenate([jnp.concatenate(tile, axis=0) for tile in tiles], axis=1)

    def summed(value):
        return (value[:, lanes_of(0)] + value[:, lanes_of(1)]) + (value[:, lanes_of(2)] + value[:, lanes_of(3)])

    for n in range(steps):
        fill_tables(seed, cos, sin, turn, n * step, (n + 1) * step)
        at = pl.ds(n * step, step)
        c_rows, s_rows = cos[at, :], sin[at, :]
        tc, ts = turn[0, at, :], turn[1, at, :]
        re, im = filt[0, at, :], filt[1, at, :]
        grad = columns(0)
        cg, sg = dot(c_rows, grad), dot(s_rows, grad)
        for q in range(SPLIT):
            a, b = cg[:, lanes_of(q)], sg[:, lanes_of(q)]
            uv[0, at, lanes_of(q)] = (a * re + b * im).astype(BF16)
            uv[1, at, lanes_of(q)] = (b * re - a * im).astype(BF16)
        mixed = columns(1)
        cm, sm = dot(c_rows, mixed), dot(s_rows, mixed)
        sum_re = summed(cg * cm + sg * sm)
        sum_im = summed(sg * cm - cg * sm) * sign
        prod[0, at, :] = (sum_re * tc + sum_im * ts).astype(BF16)
        prod[1, at, :] = (sum_re * ts - sum_im * tc).astype(BF16)

    lags = dot_tn(prod[0], cos[...]) + dot_tn(prod[1], sin[...])
    row = lax.broadcasted_iota(jnp.int32, (LANES // 2, LANES), 0)
    col = lax.broadcasted_iota(jnp.int32, (LANES // 2, LANES), 1)
    row = jnp.where(odd == 0, row, LANES // 2 - 1 - row)
    fold = jnp.where((col == row) | (col == LANES - 1 - row), 1.0, 0.0).astype(F32)
    total = jnp.dot(fold, lags * (1.0 / SEQ), precision=lax.Precision.HIGHEST, preferred_element_type=F32)
    for block in range(SEQ // BLOCK):
        folded[slot_of(z, block)] = total[:, lanes_of(block)]
    keep[...] = folded[:4]
    give[...] = folded[4:]

    leaving = []
    size = SPLIT * (step // BLOCK)
    for n in range(steps):
        at = pl.ds(n * step, step)
        value = dot(cos[at, :], uv[0]) + dot(sin[at, :], uv[1])
        value = (value * (1.0 / SEQ)).astype(BF16)
        for i in range(step // BLOCK):
            for q in range(SPLIT):
                conv[n * size + SPLIT * i + q] = value[i * BLOCK:(i + 1) * BLOCK, lanes_of(q)]
        part = pl.ds(n * size, size)
        copy = pltpu.make_async_copy(conv.at[part], conv_hbm.at[part], sem_out.at[n])
        copy.start()
        leaving.append(copy)
    for copy in leaving:
        copy.wait()


def core(place, x, filt, seed):
    part = jax.ShapeDtypeStruct((4, LANES // 2, BLOCK), F32)
    return pl.pallas_call(
        core_kernel,
        in_specs=[SMEM, VMEM, VMEM, VMEM],
        out_specs=(HBM, VMEM, VMEM),
        out_shape=(jax.ShapeDtypeStruct((GROUPS, BLOCK, LANES), BF16), part, part),
        scratch_shapes=[
            pltpu.VMEM((SEQ, SEQ), BF16),
            pltpu.VMEM((SEQ, SEQ), BF16),
            pltpu.VMEM((2, SEQ, LANES), F32),
            pltpu.VMEM((2, SEQ, WIDTH), BF16),
            pltpu.VMEM((2, SEQ, LANES), BF16),
            pltpu.VMEM((GROUPS, BLOCK, LANES), BF16),
            pltpu.VMEM((8, LANES // 2, BLOCK), F32),
            pltpu.SemaphoreType.DMA((4,)),
        ],
        compiler_params=SMALL,
        cost_estimate=pl.CostEstimate(flops=7000 * MIB, bytes_accessed=4 * MIB, transcendentals=0),
        name="core",
    )(place, x, filt, seed)


def unpack_kernel(conv, k_in, v_in, key_hbm, value_hbm, key, value, sem_out):
    tiles = GROUPS // 2 // CUTS
    width = tiles * LANES
    low = lax.broadcasted_iota(jnp.int32, (BLOCK, LANES), 1) < LANES // 2
    leaving = []
    for j in range(CUTS):
        for t in range(j * tiles, (j + 1) * tiles):
            even = conv[chunk_of(2 * t)].astype(F32)
            odd = conv[chunk_of(2 * t + 1)].astype(F32)
            ahead, behind = jnp.where(low, even, odd), jnp.where(low, odd, even)
            for cols, grad in ((lanes_of(t), ahead), (lanes_of(GROUPS - 1 - t), behind)):
                key[:, cols] = (grad * v_in[:, cols].astype(F32)).astype(BF16)
                value[:, cols] = (grad * k_in[:, cols].astype(F32)).astype(BF16)
        for s, at in enumerate((j, 2 * CUTS - 1 - j)):
            cols = pl.ds(at * width, width)
            for m, (src, dst) in enumerate(((key, key_hbm), (value, value_hbm))):
                copy = pltpu.make_async_copy(src.at[:, cols], dst.at[:, cols], sem_out.at[j, s, m])
                copy.start()
                leaving.append(copy)
    for copy in leaving:
        copy.wait()


def unpack(conv, k, v):
    shape = jax.ShapeDtypeStruct(k.shape, BF16)
    whole = pltpu.VMEM(k.shape, BF16)
    return pl.pallas_call(
        unpack_kernel,
        in_specs=[VMEM] * 3,
        out_specs=(ANY, ANY),
        out_shape=(shape, shape),
        scratch_shapes=[whole, whole, pltpu.SemaphoreType.DMA((CUTS, 2, 2))],
        compiler_params=SMALL,
        cost_estimate=pl.CostEstimate(flops=2 * MIB, bytes_accessed=5 * MIB, transcendentals=0),
        name="unpack",
    )(conv, k, v)


def times_kernel(a, b, out):
    out[...] = (a[...].astype(F32) * b[...].astype(F32)).astype(BF16)


def times(a, b):
    block = pl.BlockSpec((BLOCK // 2, a.shape[1]), lambda i: (i, 0))
    return pl.pallas_call(
        times_kernel,
        grid=(2,),
        in_specs=[block, block],
        out_specs=block,
        out_shape=jax.ShapeDtypeStruct(a.shape, BF16),
        compiler_params=SMALL,
        cost_estimate=pl.CostEstimate(flops=1, bytes_accessed=1, transcendentals=0),
        name="times",
    )(a, b)


def swap_z(block, bit):
    return lax.ppermute(block, "z", [(i, i ^ (1 << bit)) for i in range(8)])


def sent_out(filters):
    route = [(8 * l + n, 8 * OWNER[n] + LAG_AT[l]) for l in range(8) for n in range(8)]
    return lax.ppermute(filters[None], CTX_Z, route).astype(BF16)


def gathered_over_z(near):
    near = jnp.concatenate([near, swap_z(near, 2)], axis=0)
    near = jnp.concatenate([near, swap_z(near, 1)], axis=0)
    return near, swap_z(near, 0)


def summed_over_z(keep, give):
    keep = keep + swap_z(give, 0)
    keep = keep[:2] + swap_z(keep[2:], 1)
    return keep[0] + swap_z(keep[1], 2)


def sent_home(lags):
    route = [(8 * OWNER[n] + LAG_AT[l], 8 * l + n) for l in range(8) for n in range(8)]
    return lax.ppermute(lags, CTX_Z, route)


def local(query_gate, key_gate, value_in, conv_out, out_grad, filters):
    place = jnp.stack([lax.axis_index("core"), lax.axis_index("z")]).astype(jnp.int32)
    q, k, v, g = query_gate[0], key_gate[0], value_in[0], out_grad[0]
    x, near = lax.optimization_barrier((pack(q, g, k, v), sent_out(filters)))
    x = lax.all_to_all(x, PLANE, split_axis=0, concat_axis=0, tiled=True)

    near, far = gathered_over_z(near)
    filt, seed = filter_spectrum(place, near, far)
    filt, seed, query_grad = lax.optimization_barrier((filt, seed, times(g, conv_out[0])[None]))

    conv, keep, give = core(place, x, filt, seed)
    conv = lax.all_to_all(conv, PLANE, split_axis=0, concat_axis=0, tiled=True)
    lags, conv = lax.optimization_barrier((summed_over_z(keep, give), conv))
    filter_grad = sent_home(lags)
    key_grad, value_grad = unpack(conv, k, v)
    return query_grad, key_grad[None], value_grad[None], filter_grad


def solution(mesh):
    fine = Mesh(mesh.devices.reshape(2, 4, 8, 2, 2), ("xh", "y", "z", "xl", "core"))
    wide = P(("z", "xl", "core"), CTX, None)
    narrow = P(("z", "xl", "core"), CTX)
    return jax.shard_map(
        local,
        mesh=fine,
        in_specs=(wide,) * 5 + (narrow,),
        out_specs=(wide, wide, wide, narrow),
        check_vma=False,
    )
```

```python
import jax
import jax.numpy as jnp
import numpy as np
from jax import lax
from jax.experimental import pallas as pl
from jax.experimental.pallas import tpu as pltpu
from jax.sharding import Mesh
from jax.sharding import PartitionSpec as P

CTX = ("xh", "y")
PLANE = ("xh", "y", "xl", "core")
CTX_Z = ("xh", "y", "z")
SEQ = 1024
BLOCK = 128
LANES = 128
SPLIT = 4
WIDTH = SPLIT * LANES
GROUPS = 32
STEP = 32
CUTS = 4
MIB = 1024 * 1024
F32 = jnp.float32
BF16 = jnp.bfloat16


def ring(a, b, size):
    return min((a - b) % size, (b - a) % size)


def lag_homes():
    homes = []
    for n in range(8):
        far = sorted(range(8), key=lambda l: -(2 * (l // 4 != n // 4) + ring(l % 4, n % 4, 4)))
        near = sorted(range(8), key=lambda z: ring(z, n, 8))
        homes.append([near[far.index(l)] for l in range(8)])
    return homes


def slot_of(z, home):
    n = z ^ home
    return (n & 1) * 4 + (n & 2) + (n >> 2)


def dot(a, b):
    return jnp.dot(a, b, preferred_element_type=F32)


def dot_nt(a, b):
    return lax.dot_general(a, b, (((1,), (1,)), ((), ())), preferred_element_type=F32)


def dot_tn(a, b):
    return lax.dot_general(a, b, (((0,), (0,)), ((), ())), preferred_element_type=F32)


def seeds():
    odd = 2 * np.arange(SEQ, dtype=np.int64) + 1
    coarse = 2 * STEP * np.arange(SEQ // STEP, dtype=np.int64)
    fine = 2 * np.arange(STEP, dtype=np.int64) + 1
    out = []
    for part in (coarse, fine):
        angle = (np.multiply.outer(part, odd) % (8 * SEQ)).astype(np.float64) * (np.pi / (4 * SEQ))
        out += [np.cos(angle), np.sin(angle)]
    return np.stack(out).astype(np.float32)


def fill_tables(seed, cos, sin, turn, first, last):
    for a in range(first // STEP, last // STEP):
        ca, sa = seed[0, a:a + 1, :], seed[1, a:a + 1, :]
        c = ca * seed[2] - sa * seed[3]
        s = sa * seed[2] + ca * seed[3]
        rows = pl.ds(a * STEP, STEP)
        cos[rows, :] = c.astype(BF16)
        sin[rows, :] = s.astype(BF16)
        turn[0, rows, :] = jnp.broadcast_to(c[:, :1], (STEP, LANES))
        turn[1, rows, :] = jnp.broadcast_to(s[:, :1], (STEP, LANES))


def lanes_of(tile):
    return slice(tile * LANES, (tile + 1) * LANES)


def pack_kernel(q_hbm, g_hbm, k_hbm, v_hbm, x_hbm, buf, out, sem_in, sem_out):
    tiles = GROUPS // 2 // CUTS
    width = tiles * LANES
    low = lax.broadcasted_iota(jnp.int32, (BLOCK, LANES), 1) < LANES // 2
    arriving = []
    for j in range(CUTS):
        copies = []
        for i, ref in enumerate((q_hbm, g_hbm, k_hbm, v_hbm)):
            for s, at in enumerate((j, 2 * CUTS - 1 - j)):
                cols = pl.ds(at * width, width)
                copies.append(pltpu.make_async_copy(ref.at[:, cols], buf.at[i, :, cols], sem_in.at[j, i, s]))
        for copy in copies:
            copy.start()
        arriving.append(copies)
    leaving = []
    for j in range(CUTS):
        for copy in arriving[j]:
            copy.wait()
        for t in range(j * tiles, (j + 1) * tiles):
            ahead, behind = lanes_of(t), lanes_of(GROUPS - 1 - t)
            even, odd = 2 * t, 2 * t + 1
            for kind in range(2):
                a, b = 2 * kind, 2 * kind + 1
                f = buf[a, :, ahead].astype(F32) * buf[b, :, ahead].astype(F32)
                r = buf[a, :, behind].astype(F32) * buf[b, :, behind].astype(F32)
                out[even, kind] = jnp.where(low, f, r).astype(BF16)
                out[odd, kind] = jnp.where(low, r, f).astype(BF16)
            pair = pl.ds(even, 2)
            copy = pltpu.make_async_copy(out.at[pair], x_hbm.at[pair], sem_out.at[t])
            copy.start()
            leaving.append(copy)
    for copy in leaving:
        copy.wait()


ANY = pl.BlockSpec(memory_space=pl.ANY)
VMEM = pl.BlockSpec(memory_space=pltpu.VMEM)
SMEM = pl.BlockSpec(memory_space=pltpu.SMEM)
HBM = pl.BlockSpec(memory_space=pltpu.HBM)
LIMIT = pltpu.CompilerParams(vmem_limit_bytes=60 * MIB)
SMALL = pltpu.CompilerParams(vmem_limit_bytes=24 * MIB)


def pack(q, g, k, v):
    return pl.pallas_call(
        pack_kernel,
        in_specs=[ANY] * 4,
        out_specs=ANY,
        out_shape=jax.ShapeDtypeStruct((GROUPS, 2, BLOCK, LANES), BF16),
        scratch_shapes=[
            pltpu.VMEM((4,) + q.shape, BF16),
            pltpu.VMEM((GROUPS, 2, BLOCK, LANES), BF16),
            pltpu.SemaphoreType.DMA((CUTS, 4, 2)),
            pltpu.SemaphoreType.DMA((GROUPS // 2,)),
        ],
        compiler_params=LIMIT,
        cost_estimate=pl.CostEstimate(flops=2 * MIB, bytes_accessed=6 * MIB, transcendentals=0),
        name="pack",
    )(q, g, k, v)


def filter_kernel(place_ref, seed, near, far, filt_hbm, seed_out, filt, rows_in, cos, sin, turn, sem):
    odd, z = place_ref[0], place_ref[1]
    step = 256
    row = lax.broadcasted_iota(jnp.int32, (LANES, LANES // 2), 0)
    col = lax.broadcasted_iota(jnp.int32, (LANES, LANES // 2), 1)
    ahead = row - jnp.where(odd == 0, 0, LANES // 2)
    behind = jnp.where(odd == 0, LANES, LANES // 2) - 1 - row
    spread = jnp.where((col == ahead) | (col == behind), 1.0, 0.0).astype(BF16)
    for block in range(SEQ // BLOCK):
        slot = slot_of(z, place_ref[2 + block])
        lags = jnp.where(slot < 4, near[slot % 4], far[slot % 4]).astype(BF16)
        rows_in[:, lanes_of(block)] = dot(spread, lags).astype(BF16)
    sign = strand_sign(odd)
    for n in range(SEQ // step):
        fill_tables(seed, cos, sin, turn, n * step, (n + 1) * step)
        at = pl.ds(n * step, step)
        fc, fs = dot_nt(cos[at, :], rows_in[...]), dot_nt(sin[at, :], rows_in[...])
        tc, ts = turn[0, at, :], turn[1, at, :]
        filt[0, at, :] = fc * tc + fs * ts
        filt[1, at, :] = (fc * ts - fs * tc) * sign
    copy = pltpu.make_async_copy(filt, filt_hbm, sem.at[0])
    copy.start()
    seed_out[...] = seed[...]
    copy.wait()


def filter_spectrum(place, near, far):
    seed = jnp.asarray(seeds())
    return pl.pallas_call(
        filter_kernel,
        in_specs=[SMEM, VMEM, VMEM, VMEM],
        out_specs=(HBM, VMEM),
        out_shape=(pltpu.HBM((2, SEQ, LANES), F32), jax.ShapeDtypeStruct(seed.shape, F32)),
        scratch_shapes=[
            pltpu.VMEM((2, SEQ, LANES), F32),
            pltpu.VMEM((LANES, SEQ), BF16),
            pltpu.VMEM((SEQ, SEQ), BF16),
            pltpu.VMEM((SEQ, SEQ), BF16),
            pltpu.VMEM((2, SEQ, LANES), F32),
            pltpu.SemaphoreType.DMA((1,)),
        ],
        compiler_params=SMALL,
        cost_estimate=pl.CostEstimate(flops=1, bytes_accessed=1, transcendentals=0),
        name="filter_spectrum",
    )(place, seed, near, far)


def strand_sign(odd):
    lane = lax.broadcasted_iota(jnp.int32, (1, LANES), 1)
    return jnp.where((lane < LANES // 2) == (odd == 0), -1.0, 1.0).astype(F32)


def core_kernel(place_ref, x, filt_hbm, seed, keep, give, uv, cos, sin, filt, turn, prod, folded, sem_in):
    odd, z = place_ref[0], place_ref[1]
    step = 256
    steps = SEQ // step
    sign = strand_sign(odd)
    filt_copy = pltpu.make_async_copy(filt_hbm, filt, sem_in.at[0])
    filt_copy.start()
    def columns(kind):
        tiles = [[x[SPLIT * i + q, kind] for i in range(SEQ // BLOCK)] for q in range(SPLIT)]
        return jnp.concatenate([jnp.concatenate(tile, axis=0) for tile in tiles], axis=1)

    def summed(value):
        return (value[:, lanes_of(0)] + value[:, lanes_of(1)]) + (value[:, lanes_of(2)] + value[:, lanes_of(3)])

    for n in range(steps):
        fill_tables(seed, cos, sin, turn, n * step, (n + 1) * step)
        at = pl.ds(n * step, step)
        c_rows, s_rows = cos[at, :], sin[at, :]
        tc, ts = turn[0, at, :], turn[1, at, :]
        grad = columns(0)
        cg, sg = dot(c_rows, grad), dot(s_rows, grad)
        if n == 0:
            filt_copy.wait()
        re, im = filt[0, at, :], filt[1, at, :]
        for q in range(SPLIT):
            a, b = cg[:, lanes_of(q)], sg[:, lanes_of(q)]
            uv[0, at, lanes_of(q)] = (a * re + b * im).astype(BF16)
            uv[1, at, lanes_of(q)] = (b * re - a * im).astype(BF16)
        mixed = columns(1)
        cm, sm = dot(c_rows, mixed), dot(s_rows, mixed)
        sum_re = summed(cg * cm + sg * sm)
        sum_im = summed(sg * cm - cg * sm) * sign
        prod[0, at, :] = (sum_re * tc + sum_im * ts).astype(BF16)
        prod[1, at, :] = (sum_re * ts - sum_im * tc).astype(BF16)

    lags = dot_tn(prod[0], cos[...]) + dot_tn(prod[1], sin[...])
    row = lax.broadcasted_iota(jnp.int32, (LANES // 2, LANES), 0)
    col = lax.broadcasted_iota(jnp.int32, (LANES // 2, LANES), 1)
    row = jnp.where(odd == 0, row, LANES // 2 - 1 - row)
    fold = jnp.where((col == row) | (col == LANES - 1 - row), 1.0 / SEQ, 0.0).astype(BF16)
    upper = lags.astype(BF16)
    total = dot(fold, upper) + dot(fold, (lags - upper.astype(F32)).astype(BF16))
    for block in range(SEQ // BLOCK):
        home = place_ref[2 + block]
        folded[((z ^ home) & 1) * 4 + (home & 2) + (home >> 2)] = total[:, lanes_of(block)]
    keep[...] = folded[:4]
    give[...] = folded[4:].astype(BF16)


def back_kernel(uv, cos, sin, conv_hbm, conv, sem_out):
    step = 256
    steps = SEQ // step
    leaving = []
    size = SPLIT * (step // BLOCK)
    for n in range(steps):
        at = pl.ds(n * step, step)
        value = dot(cos[at, :], uv[0]) + dot(sin[at, :], uv[1])
        value = (value * (1.0 / SEQ)).astype(BF16)
        for i in range(step // BLOCK):
            for q in range(SPLIT):
                conv[n * size + SPLIT * i + q] = value[i * BLOCK:(i + 1) * BLOCK, lanes_of(q)]
        part = pl.ds(n * size, size)
        copy = pltpu.make_async_copy(conv.at[part], conv_hbm.at[part], sem_out.at[n])
        copy.start()
        leaving.append(copy)
    for copy in leaving:
        copy.wait()


def core(place, x, filt, seed):
    table = pltpu.VMEM((SEQ, SEQ), BF16)
    return pl.pallas_call(
        core_kernel,
        in_specs=[SMEM, VMEM, HBM, VMEM],
        out_specs=(VMEM,) * 5,
        out_shape=(
            jax.ShapeDtypeStruct((4, LANES // 2, BLOCK), F32),
            jax.ShapeDtypeStruct((4, LANES // 2, BLOCK), BF16),
            pltpu.VMEM((2, SEQ, WIDTH), BF16),
            table,
            table,
        ),
        scratch_shapes=[
            pltpu.VMEM((2, SEQ, LANES), F32),
            pltpu.VMEM((2, SEQ, LANES), F32),
            pltpu.VMEM((2, SEQ, LANES), BF16),
            pltpu.VMEM((8, LANES // 2, BLOCK), F32),
            pltpu.SemaphoreType.DMA((1,)),
        ],
        compiler_params=SMALL,
        cost_estimate=pl.CostEstimate(flops=5000 * MIB, bytes_accessed=4 * MIB, transcendentals=0),
        name="core",
    )(place, x, pltpu.with_memory_space_constraint(filt, pltpu.HBM), seed)


def back(uv, cos, sin):
    return pl.pallas_call(
        back_kernel,
        in_specs=[VMEM] * 3,
        out_specs=HBM,
        out_shape=pltpu.HBM((GROUPS, BLOCK, LANES), BF16),
        scratch_shapes=[pltpu.VMEM((GROUPS, BLOCK, LANES), BF16), pltpu.SemaphoreType.DMA((4,))],
        compiler_params=SMALL,
        cost_estimate=pl.CostEstimate(flops=2100 * MIB, bytes_accessed=MIB, transcendentals=0),
        name="back",
    )(uv, cos, sin)


def unpack_kernel(conv, k_in, v_in, lags, key_hbm, value_hbm, lags_hbm, key, value, sem_out, sem_lags):
    tiles = GROUPS // 2 // CUTS
    width = tiles * LANES
    lags_copy = pltpu.make_async_copy(lags, lags_hbm, sem_lags.at[0])
    lags_copy.start()
    low = lax.broadcasted_iota(jnp.int32, (BLOCK, LANES), 1) < LANES // 2
    leaving = []
    for j in range(CUTS):
        for t in range(j * tiles, (j + 1) * tiles):
            even = conv[2 * t].astype(F32)
            odd = conv[2 * t + 1].astype(F32)
            ahead, behind = jnp.where(low, even, odd), jnp.where(low, odd, even)
            for cols, grad in ((lanes_of(t), ahead), (lanes_of(GROUPS - 1 - t), behind)):
                key[:, cols] = (grad * v_in[:, cols].astype(F32)).astype(BF16)
                value[:, cols] = (grad * k_in[:, cols].astype(F32)).astype(BF16)
        for s, at in enumerate((j, 2 * CUTS - 1 - j)):
            cols = pl.ds(at * width, width)
            for m, (src, dst) in enumerate(((key, key_hbm), (value, value_hbm))):
                copy = pltpu.make_async_copy(src.at[:, cols], dst.at[:, cols], sem_out.at[j, s, m])
                copy.start()
                leaving.append(copy)
    lags_copy.wait()
    for copy in leaving:
        copy.wait()


def unpack(conv, k, v, lags):
    shape = jax.ShapeDtypeStruct(k.shape, BF16)
    whole = pltpu.VMEM(k.shape, BF16)
    return pl.pallas_call(
        unpack_kernel,
        in_specs=[VMEM] * 4,
        out_specs=(ANY,) * 3,
        out_shape=(shape, shape, jax.ShapeDtypeStruct(lags.shape, F32)),
        scratch_shapes=[whole, whole, pltpu.SemaphoreType.DMA((CUTS, 2, 2)), pltpu.SemaphoreType.DMA((1,))],
        compiler_params=SMALL,
        cost_estimate=pl.CostEstimate(flops=2 * MIB, bytes_accessed=5 * MIB, transcendentals=0),
        name="unpack",
    )(conv, k, v, lags)


def times_kernel(a, b, out):
    out[...] = (a[...].astype(F32) * b[...].astype(F32)).astype(BF16)


def times(a, b):
    block = pl.BlockSpec((BLOCK // 2, a.shape[1]), lambda i: (i, 0))
    return pl.pallas_call(
        times_kernel,
        grid=(2,),
        in_specs=[block, block],
        out_specs=block,
        out_shape=jax.ShapeDtypeStruct(a.shape, BF16),
        compiler_params=SMALL,
        cost_estimate=pl.CostEstimate(flops=1, bytes_accessed=1, transcendentals=0),
        name="times",
    )(a, b)


def swap_z(block, bit):
    return lax.ppermute(block, "z", [(i, i ^ (1 << bit)) for i in range(8)])


def sent_out(filters):
    homes = lag_homes()
    route = [(8 * l + n, 8 * n + homes[n][l]) for l in range(8) for n in range(8)]
    return lax.ppermute(filters, CTX_Z, route)[None]


def gathered_over_z(near):
    near = jnp.concatenate([near, swap_z(near, 2)], axis=0)
    near = jnp.concatenate([near, swap_z(near, 1)], axis=0)
    return near, swap_z(near, 0)


def summed_over_z(lags, bit):
    low, high = jnp.split(lags, 2, axis=0)
    first = (lax.axis_index("z") >> bit) % 2 == 0
    given = jnp.where(first, high, low).astype(BF16)
    return jnp.where(first, low, high) + swap_z(given, bit).astype(F32)


def sent_home(lags):
    homes = lag_homes()
    route = [(8 * n + homes[n][l], 8 * l + n) for l in range(8) for n in range(8)]
    return lax.ppermute(lags, CTX_Z, route)


def local(query_gate, key_gate, value_in, conv_out, out_grad, filters):
    home = jnp.asarray(lag_homes(), jnp.int32)[lax.axis_index(CTX)]
    place = jnp.concatenate([jnp.stack([lax.axis_index("core"), lax.axis_index("z")]).astype(jnp.int32), home])
    q, k, v, g = query_gate[0], key_gate[0], value_in[0], out_grad[0]
    x, near = lax.optimization_barrier((pack(q, g, k, v), sent_out(filters)))
    x = lax.all_to_all(x, PLANE, split_axis=0, concat_axis=0, tiled=True)

    near, far = gathered_over_z(near)
    filt, seed = filter_spectrum(place, near, far)
    filt, seed, query_grad = lax.optimization_barrier((filt, seed, times(g, conv_out[0])[None]))

    keep, give, uv, cos, sin = core(place, x, filt, seed)
    lags = keep + swap_z(give, 0).astype(F32)
    conv = lax.all_to_all(back(uv, cos, sin), PLANE, split_axis=0, concat_axis=0, tiled=True)
    lags = summed_over_z(summed_over_z(lags, 1), 2)[0]
    key_grad, value_grad, filter_grad = unpack(conv, k, v, sent_home(lags))
    return query_grad, key_grad[None], value_grad[None], filter_grad


def solution(mesh):
    fine = Mesh(mesh.devices.reshape(2, 4, 8, 2, 2), ("xh", "y", "z", "xl", "core"))
    wide = P(("z", "xl", "core"), CTX, None)
    narrow = P(("z", "xl", "core"), CTX)
    return jax.shard_map(
        local,
        mesh=fine,
        in_specs=(wide,) * 5 + (narrow,),
        out_specs=(wide, wide, wide, narrow),
        check_vma=False,
    )
```

```python
import jax
import jax.numpy as jnp
import numpy as np
from jax import lax
from jax.experimental import pallas as pl
from jax.experimental.pallas import tpu as pltpu
from jax.sharding import Mesh
from jax.sharding import PartitionSpec as P

CTX = ("xh", "y")
PLANE = ("xh", "y", "xl", "core")
CTX_Z = ("xh", "y", "z")
SEQ = 1024
BLOCK = 128
LANES = 128
SPLIT = 4
WIDTH = SPLIT * LANES
GROUPS = 32
STEP = 32
CUTS = 4
MIB = 1024 * 1024
F32 = jnp.float32
BF16 = jnp.bfloat16


def ring(a, b, size):
    return min((a - b) % size, (b - a) % size)


def lag_homes():
    homes = []
    for n in range(8):
        far = sorted(range(8), key=lambda l: -(2 * (l // 4 != n // 4) + ring(l % 4, n % 4, 4)))
        near = sorted(range(8), key=lambda z: ring(z, n, 8))
        homes.append([near[far.index(l)] for l in range(8)])
    return homes


def slot_of(z, home):
    n = z ^ home
    return (n & 1) * 4 + (n & 2) + (n >> 2)


def dot(a, b):
    return jnp.dot(a, b, preferred_element_type=F32)


def dot_nt(a, b):
    return lax.dot_general(a, b, (((1,), (1,)), ((), ())), preferred_element_type=F32)


def dot_tn(a, b):
    return lax.dot_general(a, b, (((0,), (0,)), ((), ())), preferred_element_type=F32)


def seeds():
    odd = 2 * np.arange(SEQ, dtype=np.int64) + 1
    coarse = 2 * STEP * np.arange(SEQ // STEP, dtype=np.int64)
    fine = 2 * np.arange(STEP, dtype=np.int64) + 1
    out = []
    for part in (coarse, fine):
        angle = (np.multiply.outer(part, odd) % (8 * SEQ)).astype(np.float64) * (np.pi / (4 * SEQ))
        out += [np.cos(angle), np.sin(angle)]
    return np.stack(out).astype(np.float32)


def fill_tables(seed, cos, sin, turn, first, last):
    for a in range(first // STEP, last // STEP):
        ca, sa = seed[0, a:a + 1, :], seed[1, a:a + 1, :]
        c = ca * seed[2] - sa * seed[3]
        s = sa * seed[2] + ca * seed[3]
        rows = pl.ds(a * STEP, STEP)
        cos[rows, :] = c.astype(BF16)
        sin[rows, :] = s.astype(BF16)
        turn[0, rows, :] = jnp.broadcast_to(c[:, :1], (STEP, LANES))
        turn[1, rows, :] = jnp.broadcast_to(s[:, :1], (STEP, LANES))


def lanes_of(tile):
    return slice(tile * LANES, (tile + 1) * LANES)


def pack_kernel(q_hbm, g_hbm, k_hbm, v_hbm, x_hbm, buf, out, sem_in, sem_out):
    tiles = GROUPS // 2 // CUTS
    width = tiles * LANES
    low = lax.broadcasted_iota(jnp.int32, (BLOCK, LANES), 1) < LANES // 2
    arriving = []
    for j in range(CUTS):
        copies = []
        for i, ref in enumerate((q_hbm, g_hbm, k_hbm, v_hbm)):
            for s, at in enumerate((j, 2 * CUTS - 1 - j)):
                cols = pl.ds(at * width, width)
                copies.append(pltpu.make_async_copy(ref.at[:, cols], buf.at[i, :, cols], sem_in.at[j, i, s]))
        for copy in copies:
            copy.start()
        arriving.append(copies)
    leaving = []
    for j in range(CUTS):
        for copy in arriving[j]:
            copy.wait()
        for t in range(j * tiles, (j + 1) * tiles):
            ahead, behind = lanes_of(t), lanes_of(GROUPS - 1 - t)
            even, odd = 2 * t, 2 * t + 1
            for kind in range(2):
                a, b = 2 * kind, 2 * kind + 1
                f = buf[a, :, ahead].astype(F32) * buf[b, :, ahead].astype(F32)
                r = buf[a, :, behind].astype(F32) * buf[b, :, behind].astype(F32)
                out[even, kind] = jnp.where(low, f, r).astype(BF16)
                out[odd, kind] = jnp.where(low, r, f).astype(BF16)
            pair = pl.ds(even, 2)
            copy = pltpu.make_async_copy(out.at[pair], x_hbm.at[pair], sem_out.at[t])
            copy.start()
            leaving.append(copy)
    for copy in leaving:
        copy.wait()


ANY = pl.BlockSpec(memory_space=pl.ANY)
VMEM = pl.BlockSpec(memory_space=pltpu.VMEM)
SMEM = pl.BlockSpec(memory_space=pltpu.SMEM)
HBM = pl.BlockSpec(memory_space=pltpu.HBM)
LIMIT = pltpu.CompilerParams(vmem_limit_bytes=60 * MIB)
SMALL = pltpu.CompilerParams(vmem_limit_bytes=24 * MIB)


def pack(q, g, k, v):
    return pl.pallas_call(
        pack_kernel,
        in_specs=[ANY] * 4,
        out_specs=ANY,
        out_shape=jax.ShapeDtypeStruct((GROUPS, 2, BLOCK, LANES), BF16),
        scratch_shapes=[
            pltpu.VMEM((4,) + q.shape, BF16),
            pltpu.VMEM((GROUPS, 2, BLOCK, LANES), BF16),
            pltpu.SemaphoreType.DMA((CUTS, 4, 2)),
            pltpu.SemaphoreType.DMA((GROUPS // 2,)),
        ],
        compiler_params=LIMIT,
        cost_estimate=pl.CostEstimate(flops=2 * MIB, bytes_accessed=6 * MIB, transcendentals=0),
        name="pack",
    )(q, g, k, v)


def filter_kernel(place_ref, seed, near, far, filt_hbm, seed_out, filt, rows_in, cos, sin, turn, sem):
    odd, z = place_ref[0], place_ref[1]
    step = 256
    row = lax.broadcasted_iota(jnp.int32, (LANES, LANES // 2), 0)
    col = lax.broadcasted_iota(jnp.int32, (LANES, LANES // 2), 1)
    ahead = row - jnp.where(odd == 0, 0, LANES // 2)
    behind = jnp.where(odd == 0, LANES, LANES // 2) - 1 - row
    spread = jnp.where((col == ahead) | (col == behind), 1.0, 0.0).astype(BF16)
    for block in range(SEQ // BLOCK):
        slot = slot_of(z, place_ref[2 + block])
        lags = jnp.where(slot < 4, near[slot % 4], far[slot % 4]).astype(BF16)
        rows_in[:, lanes_of(block)] = dot(spread, lags).astype(BF16)
    sign = strand_sign(odd)
    for n in range(SEQ // step):
        fill_tables(seed, cos, sin, turn, n * step, (n + 1) * step)
        at = pl.ds(n * step, step)
        fc, fs = dot_nt(cos[at, :], rows_in[...]), dot_nt(sin[at, :], rows_in[...])
        tc, ts = turn[0, at, :], turn[1, at, :]
        filt[0, at, :] = fc * tc + fs * ts
        filt[1, at, :] = (fc * ts - fs * tc) * sign
    copy = pltpu.make_async_copy(filt, filt_hbm, sem.at[0])
    copy.start()
    seed_out[...] = seed[...]
    copy.wait()


def filter_spectrum(place, near, far):
    seed = jnp.asarray(seeds())
    return pl.pallas_call(
        filter_kernel,
        in_specs=[SMEM, VMEM, VMEM, VMEM],
        out_specs=(HBM, VMEM),
        out_shape=(pltpu.HBM((2, SEQ, LANES), F32), jax.ShapeDtypeStruct(seed.shape, F32)),
        scratch_shapes=[
            pltpu.VMEM((2, SEQ, LANES), F32),
            pltpu.VMEM((LANES, SEQ), BF16),
            pltpu.VMEM((SEQ, SEQ), BF16),
            pltpu.VMEM((SEQ, SEQ), BF16),
            pltpu.VMEM((2, SEQ, LANES), F32),
            pltpu.SemaphoreType.DMA((1,)),
        ],
        compiler_params=SMALL,
        cost_estimate=pl.CostEstimate(flops=1, bytes_accessed=1, transcendentals=0),
        name="filter_spectrum",
    )(place, seed, near, far)


def strand_sign(odd):
    lane = lax.broadcasted_iota(jnp.int32, (1, LANES), 1)
    return jnp.where((lane < LANES // 2) == (odd == 0), -1.0, 1.0).astype(F32)


def core_kernel(place_ref, x, filt_hbm, seed, keep, give, uv, cos, sin, filt, turn, prod, folded, sem_in):
    odd, z = place_ref[0], place_ref[1]
    step = 256
    steps = SEQ // step
    sign = strand_sign(odd)
    filt_copy = pltpu.make_async_copy(filt_hbm, filt, sem_in.at[0])
    filt_copy.start()
    def columns(kind):
        tiles = [[x[SPLIT * i + q, kind] for i in range(SEQ // BLOCK)] for q in range(SPLIT)]
        return jnp.concatenate([jnp.concatenate(tile, axis=0) for tile in tiles], axis=1)

    def summed(value):
        return (value[:, lanes_of(0)] + value[:, lanes_of(1)]) + (value[:, lanes_of(2)] + value[:, lanes_of(3)])

    for n in range(steps):
        fill_tables(seed, cos, sin, turn, n * step, (n + 1) * step)
        at = pl.ds(n * step, step)
        c_rows, s_rows = cos[at, :], sin[at, :]
        tc, ts = turn[0, at, :], turn[1, at, :]
        grad = columns(0)
        cg, sg = dot(c_rows, grad), dot(s_rows, grad)
        if n == 0:
            filt_copy.wait()
        re, im = filt[0, at, :], filt[1, at, :]
        for q in range(SPLIT):
            a, b = cg[:, lanes_of(q)], sg[:, lanes_of(q)]
            uv[0, at, lanes_of(q)] = (a * re + b * im).astype(BF16)
            uv[1, at, lanes_of(q)] = (b * re - a * im).astype(BF16)
        mixed = columns(1)
        cm, sm = dot(c_rows, mixed), dot(s_rows, mixed)
        sum_re = summed(cg * cm + sg * sm)
        sum_im = summed(sg * cm - cg * sm) * sign
        prod[0, at, :] = (sum_re * tc + sum_im * ts).astype(BF16)
        prod[1, at, :] = (sum_re * ts - sum_im * tc).astype(BF16)

    lags = dot_tn(prod[0], cos[...]) + dot_tn(prod[1], sin[...])
    row = lax.broadcasted_iota(jnp.int32, (LANES // 2, LANES), 0)
    col = lax.broadcasted_iota(jnp.int32, (LANES // 2, LANES), 1)
    row = jnp.where(odd == 0, row, LANES // 2 - 1 - row)
    fold = jnp.where((col == row) | (col == LANES - 1 - row), 1.0, 0.0).astype(BF16)
    upper = lags.astype(BF16)
    total = dot(fold, upper) + dot(fold, (lags - upper.astype(F32)).astype(BF16))
    for block in range(SEQ // BLOCK):
        home = place_ref[2 + block]
        folded[((z ^ home) & 2) * 2 + (home & 1) * 2 + (home >> 2)] = total[:, lanes_of(block)]
    keep[...] = folded[:4]
    give[...] = folded[4:].astype(BF16)


def back_kernel(uv, cos, sin, conv_hbm, conv, sem_out):
    step = 256
    steps = SEQ // step
    leaving = []
    size = SPLIT * (step // BLOCK)
    for n in range(steps):
        at = pl.ds(n * step, step)
        value = dot(cos[at, :], uv[0]) + dot(sin[at, :], uv[1])
        value = (value * (1.0 / SEQ)).astype(BF16)
        for i in range(step // BLOCK):
            for q in range(SPLIT):
                conv[n * size + SPLIT * i + q] = value[i * BLOCK:(i + 1) * BLOCK, lanes_of(q)]
        part = pl.ds(n * size, size)
        copy = pltpu.make_async_copy(conv.at[part], conv_hbm.at[part], sem_out.at[n])
        copy.start()
        leaving.append(copy)
    for copy in leaving:
        copy.wait()


def core(place, x, filt, seed):
    table = pltpu.VMEM((SEQ, SEQ), BF16)
    return pl.pallas_call(
        core_kernel,
        in_specs=[SMEM, VMEM, HBM, VMEM],
        out_specs=(VMEM,) * 5,
        out_shape=(
            jax.ShapeDtypeStruct((4, LANES // 2, BLOCK), F32),
            jax.ShapeDtypeStruct((4, LANES // 2, BLOCK), BF16),
            pltpu.VMEM((2, SEQ, WIDTH), BF16),
            table,
            table,
        ),
        scratch_shapes=[
            pltpu.VMEM((2, SEQ, LANES), F32),
            pltpu.VMEM((2, SEQ, LANES), F32),
            pltpu.VMEM((2, SEQ, LANES), BF16),
            pltpu.VMEM((8, LANES // 2, BLOCK), F32),
            pltpu.SemaphoreType.DMA((1,)),
        ],
        compiler_params=SMALL,
        cost_estimate=pl.CostEstimate(flops=5000 * MIB, bytes_accessed=4 * MIB, transcendentals=0),
        name="core",
    )(place, x, pltpu.with_memory_space_constraint(filt, pltpu.HBM), seed)


def back(uv, cos, sin):
    return pl.pallas_call(
        back_kernel,
        in_specs=[VMEM] * 3,
        out_specs=HBM,
        out_shape=pltpu.HBM((GROUPS, BLOCK, LANES), BF16),
        scratch_shapes=[pltpu.VMEM((GROUPS, BLOCK, LANES), BF16), pltpu.SemaphoreType.DMA((4,))],
        compiler_params=SMALL,
        cost_estimate=pl.CostEstimate(flops=2100 * MIB, bytes_accessed=MIB, transcendentals=0),
        name="back",
    )(uv, cos, sin)


def unpack_kernel(conv, k_in, v_in, lags, key_hbm, value_hbm, lags_hbm, key, value, sem_out, sem_lags):
    tiles = GROUPS // 2 // CUTS
    width = tiles * LANES
    lags_copy = pltpu.make_async_copy(lags, lags_hbm, sem_lags.at[0])
    lags_copy.start()
    low = lax.broadcasted_iota(jnp.int32, (BLOCK, LANES), 1) < LANES // 2
    leaving = []
    for j in range(CUTS):
        for t in range(j * tiles, (j + 1) * tiles):
            even = conv[2 * t].astype(F32)
            odd = conv[2 * t + 1].astype(F32)
            ahead, behind = jnp.where(low, even, odd), jnp.where(low, odd, even)
            for cols, grad in ((lanes_of(t), ahead), (lanes_of(GROUPS - 1 - t), behind)):
                key[:, cols] = (grad * v_in[:, cols].astype(F32)).astype(BF16)
                value[:, cols] = (grad * k_in[:, cols].astype(F32)).astype(BF16)
        for s, at in enumerate((j, 2 * CUTS - 1 - j)):
            cols = pl.ds(at * width, width)
            for m, (src, dst) in enumerate(((key, key_hbm), (value, value_hbm))):
                copy = pltpu.make_async_copy(src.at[:, cols], dst.at[:, cols], sem_out.at[j, s, m])
                copy.start()
                leaving.append(copy)
    lags_copy.wait()
    for copy in leaving:
        copy.wait()


def unpack(conv, k, v, lags):
    shape = jax.ShapeDtypeStruct(k.shape, BF16)
    whole = pltpu.VMEM(k.shape, BF16)
    return pl.pallas_call(
        unpack_kernel,
        in_specs=[VMEM] * 4,
        out_specs=(ANY,) * 3,
        out_shape=(shape, shape, jax.ShapeDtypeStruct(lags.shape, F32)),
        scratch_shapes=[whole, whole, pltpu.SemaphoreType.DMA((CUTS, 2, 2)), pltpu.SemaphoreType.DMA((1,))],
        compiler_params=SMALL,
        cost_estimate=pl.CostEstimate(flops=2 * MIB, bytes_accessed=5 * MIB, transcendentals=0),
        name="unpack",
    )(conv, k, v, lags)


def times_kernel(a, b, out):
    out[...] = (a[...].astype(F32) * b[...].astype(F32)).astype(BF16)


def times(a, b):
    block = pl.BlockSpec((BLOCK // 2, a.shape[1]), lambda i: (i, 0))
    return pl.pallas_call(
        times_kernel,
        grid=(2,),
        in_specs=[block, block],
        out_specs=block,
        out_shape=jax.ShapeDtypeStruct(a.shape, BF16),
        compiler_params=SMALL,
        cost_estimate=pl.CostEstimate(flops=1, bytes_accessed=1, transcendentals=0),
        name="times",
    )(a, b)


def swap_z(block, bit):
    return lax.ppermute(block, "z", [(i, i ^ (1 << bit)) for i in range(8)])


def sent_out(filters):
    homes = lag_homes()
    route = [(8 * l + n, 8 * n + homes[n][l]) for l in range(8) for n in range(8)]
    return lax.ppermute(filters, CTX_Z, route)[None]


def gathered_over_z(near):
    near = jnp.concatenate([near, swap_z(near, 2)], axis=0)
    near = jnp.concatenate([near, swap_z(near, 1)], axis=0)
    return near, swap_z(near, 0)


def halves(lags, bit):
    low, high = jnp.split(lags, 2, axis=0)
    first = (lax.axis_index("z") >> bit) % 2 == 0
    kept = lax.optimization_barrier(jnp.where(first, low, high))
    given = lax.optimization_barrier(jnp.where(first, high, low))
    return kept, given.astype(BF16)


def joined(kept, given, bit):
    other = lax.optimization_barrier(swap_z(given, bit).astype(F32))
    total = lax.optimization_barrier(kept + other)
    for halvings in (3, 2):
        total = lax.optimization_barrier(total * 0.5**halvings)
    return total


def sent_home(lags):
    homes = lag_homes()
    route = [(8 * n + homes[n][l], 8 * l + n) for l in range(8) for n in range(8)]
    return lax.ppermute(lags, CTX_Z, route)


def local(query_gate, key_gate, value_in, conv_out, out_grad, filters):
    home = jnp.asarray(lag_homes(), jnp.int32)[lax.axis_index(CTX)]
    place = jnp.concatenate([jnp.stack([lax.axis_index("core"), lax.axis_index("z")]).astype(jnp.int32), home])
    q, k, v, g = query_gate[0], key_gate[0], value_in[0], out_grad[0]
    x, near = lax.optimization_barrier((pack(q, g, k, v), sent_out(filters)))
    x = lax.all_to_all(x, PLANE, split_axis=0, concat_axis=0, tiled=True)

    near, far = gathered_over_z(near)
    filt, seed = filter_spectrum(place, near, far)
    filt, seed, query_grad = lax.optimization_barrier((filt, seed, times(g, conv_out[0])[None]))

    keep, give, uv, cos, sin = core(place, x, filt, seed)
    kept, given = halves(keep + swap_z(give, 1).astype(F32), 0)
    conv, kept, given = lax.optimization_barrier((back(uv, cos, sin), kept, given))
    conv = lax.all_to_all(conv, PLANE, split_axis=0, concat_axis=0, tiled=True)
    kept, given = halves(joined(kept, given, 0), 2)
    lags = joined(kept, given, 2)[0]
    key_grad, value_grad, filter_grad = unpack(conv, k, v, sent_home(lags))
    return query_grad, key_grad[None], value_grad[None], filter_grad


def solution(mesh):
    fine = Mesh(mesh.devices.reshape(2, 4, 8, 2, 2), ("xh", "y", "z", "xl", "core"))
    wide = P(("z", "xl", "core"), CTX, None)
    narrow = P(("z", "xl", "core"), CTX)
    return jax.shard_map(
        local,
        mesh=fine,
        in_specs=(wide,) * 5 + (narrow,),
        out_specs=(wide, wide, wide, narrow),
        check_vma=False,
    )
```

```python
import jax
import jax.numpy as jnp
import numpy as np
from jax import lax
from jax.experimental import pallas as pl
from jax.experimental.pallas import tpu as pltpu
from jax.sharding import Mesh
from jax.sharding import PartitionSpec as P

CTX = ("xh", "y")
PLANE = ("xh", "y", "xl", "core")
CTX_Z = ("xh", "y", "z")
SEQ = 1024
BLOCK = 128
LANES = 128
SPLIT = 4
WIDTH = SPLIT * LANES
GROUPS = 32
STEP = 32
CUTS = 4
MIB = 1024 * 1024
F32 = jnp.float32
BF16 = jnp.bfloat16


def ring(a, b, size):
    return min((a - b) % size, (b - a) % size)


def lag_homes():
    homes = []
    for n in range(8):
        far = sorted(range(8), key=lambda l: -(2 * (l // 4 != n // 4) + ring(l % 4, n % 4, 4)))
        near = sorted(range(8), key=lambda z: ring(z, n, 8))
        homes.append([near[far.index(l)] for l in range(8)])
    return homes


def slot_of(z, home):
    n = z ^ home
    return (n & 1) * 4 + (n & 2) + (n >> 2)


def dot(a, b):
    return jnp.dot(a, b, preferred_element_type=F32)


def dot_nt(a, b):
    return lax.dot_general(a, b, (((1,), (1,)), ((), ())), preferred_element_type=F32)


def dot_tn(a, b):
    return lax.dot_general(a, b, (((0,), (0,)), ((), ())), preferred_element_type=F32)


def seeds():
    odd = 2 * np.arange(SEQ, dtype=np.int64) + 1
    coarse = 2 * STEP * np.arange(SEQ // STEP, dtype=np.int64)
    fine = 2 * np.arange(STEP, dtype=np.int64) + 1
    out = []
    for part in (coarse, fine):
        angle = (np.multiply.outer(part, odd) % (8 * SEQ)).astype(np.float64) * (np.pi / (4 * SEQ))
        out += [np.cos(angle), np.sin(angle)]
    return np.stack(out).astype(np.float32)


def fill_tables(seed, cos, sin, turn, first, last):
    for a in range(first // STEP, last // STEP):
        ca, sa = seed[0, a:a + 1, :], seed[1, a:a + 1, :]
        c = ca * seed[2] - sa * seed[3]
        s = sa * seed[2] + ca * seed[3]
        rows = pl.ds(a * STEP, STEP)
        cos[rows, :] = c.astype(BF16)
        sin[rows, :] = s.astype(BF16)
        turn[0, rows, :] = jnp.broadcast_to(c[:, :1], (STEP, LANES))
        turn[1, rows, :] = jnp.broadcast_to(s[:, :1], (STEP, LANES))


def lanes_of(tile):
    return slice(tile * LANES, (tile + 1) * LANES)


def pack_kernel(q_hbm, g_hbm, k_hbm, v_hbm, x_hbm, buf, out, sem_in, sem_out):
    tiles = GROUPS // 2 // CUTS
    width = tiles * LANES
    low = lax.broadcasted_iota(jnp.int32, (BLOCK, LANES), 1) < LANES // 2
    arriving = []
    for j in range(CUTS):
        copies = []
        for i, ref in enumerate((q_hbm, g_hbm, k_hbm, v_hbm)):
            for s, at in enumerate((j, 2 * CUTS - 1 - j)):
                cols = pl.ds(at * width, width)
                copies.append(pltpu.make_async_copy(ref.at[:, cols], buf.at[i, :, cols], sem_in.at[j, i, s]))
        for copy in copies:
            copy.start()
        arriving.append(copies)
    leaving = []
    for j in range(CUTS):
        for copy in arriving[j]:
            copy.wait()
        for t in range(j * tiles, (j + 1) * tiles):
            ahead, behind = lanes_of(t), lanes_of(GROUPS - 1 - t)
            even, odd = 2 * t, 2 * t + 1
            for kind in range(2):
                a, b = 2 * kind, 2 * kind + 1
                f = buf[a, :, ahead].astype(F32) * buf[b, :, ahead].astype(F32)
                r = buf[a, :, behind].astype(F32) * buf[b, :, behind].astype(F32)
                out[even, kind] = jnp.where(low, f, r).astype(BF16)
                out[odd, kind] = jnp.where(low, r, f).astype(BF16)
            pair = pl.ds(even, 2)
            copy = pltpu.make_async_copy(out.at[pair], x_hbm.at[pair], sem_out.at[t])
            copy.start()
            leaving.append(copy)
    for copy in leaving:
        copy.wait()


ANY = pl.BlockSpec(memory_space=pl.ANY)
VMEM = pl.BlockSpec(memory_space=pltpu.VMEM)
SMEM = pl.BlockSpec(memory_space=pltpu.SMEM)
HBM = pl.BlockSpec(memory_space=pltpu.HBM)
LIMIT = pltpu.CompilerParams(vmem_limit_bytes=60 * MIB)
SMALL = pltpu.CompilerParams(vmem_limit_bytes=24 * MIB)


def pack(q, g, k, v):
    return pl.pallas_call(
        pack_kernel,
        in_specs=[ANY] * 4,
        out_specs=ANY,
        out_shape=jax.ShapeDtypeStruct((GROUPS, 2, BLOCK, LANES), BF16),
        scratch_shapes=[
            pltpu.VMEM((4,) + q.shape, BF16),
            pltpu.VMEM((GROUPS, 2, BLOCK, LANES), BF16),
            pltpu.SemaphoreType.DMA((CUTS, 4, 2)),
            pltpu.SemaphoreType.DMA((GROUPS // 2,)),
        ],
        compiler_params=LIMIT,
        cost_estimate=pl.CostEstimate(flops=2 * MIB, bytes_accessed=6 * MIB, transcendentals=0),
        name="pack",
    )(q, g, k, v)


def filter_kernel(place_ref, seed, near, far, filt_hbm, seed_out, filt, rows_in, cos, sin, turn, sem):
    odd, z = place_ref[0], place_ref[1]
    step = 256
    row = lax.broadcasted_iota(jnp.int32, (LANES, LANES // 2), 0)
    col = lax.broadcasted_iota(jnp.int32, (LANES, LANES // 2), 1)
    ahead = row - jnp.where(odd == 0, 0, LANES // 2)
    behind = jnp.where(odd == 0, LANES, LANES // 2) - 1 - row
    spread = jnp.where((col == ahead) | (col == behind), 1.0, 0.0).astype(BF16)
    for block in range(SEQ // BLOCK):
        slot = slot_of(z, place_ref[2 + block])
        lags = jnp.where(slot < 4, near[slot % 4], far[slot % 4]).astype(BF16)
        rows_in[:, lanes_of(block)] = dot(spread, lags).astype(BF16)
    sign = strand_sign(odd)
    for n in range(SEQ // step):
        fill_tables(seed, cos, sin, turn, n * step, (n + 1) * step)
        at = pl.ds(n * step, step)
        fc, fs = dot_nt(cos[at, :], rows_in[...]), dot_nt(sin[at, :], rows_in[...])
        tc, ts = turn[0, at, :], turn[1, at, :]
        filt[0, at, :] = fc * tc + fs * ts
        filt[1, at, :] = (fc * ts - fs * tc) * sign
    copy = pltpu.make_async_copy(filt, filt_hbm, sem.at[0])
    copy.start()
    seed_out[...] = seed[...]
    copy.wait()


def filter_spectrum(place, near, far):
    seed = jnp.asarray(seeds())
    return pl.pallas_call(
        filter_kernel,
        in_specs=[SMEM, VMEM, VMEM, VMEM],
        out_specs=(HBM, VMEM),
        out_shape=(pltpu.HBM((2, SEQ, LANES), F32), jax.ShapeDtypeStruct(seed.shape, F32)),
        scratch_shapes=[
            pltpu.VMEM((2, SEQ, LANES), F32),
            pltpu.VMEM((LANES, SEQ), BF16),
            pltpu.VMEM((SEQ, SEQ), BF16),
            pltpu.VMEM((SEQ, SEQ), BF16),
            pltpu.VMEM((2, SEQ, LANES), F32),
            pltpu.SemaphoreType.DMA((1,)),
        ],
        compiler_params=SMALL,
        cost_estimate=pl.CostEstimate(flops=1, bytes_accessed=1, transcendentals=0),
        name="filter_spectrum",
    )(place, seed, near, far)


def strand_sign(odd):
    lane = lax.broadcasted_iota(jnp.int32, (1, LANES), 1)
    return jnp.where((lane < LANES // 2) == (odd == 0), -1.0, 1.0).astype(F32)


def core_kernel(place_ref, x, filt_hbm, seed, keep, give, uv, cos, sin, filt, turn, prod, folded, sem_in):
    odd, z = place_ref[0], place_ref[1]
    step = 256
    steps = SEQ // step
    sign = strand_sign(odd)
    filt_copy = pltpu.make_async_copy(filt_hbm, filt, sem_in.at[0])
    filt_copy.start()
    def columns(kind):
        tiles = [[x[SPLIT * i + q, kind] for i in range(SEQ // BLOCK)] for q in range(SPLIT)]
        return jnp.concatenate([jnp.concatenate(tile, axis=0) for tile in tiles], axis=1)

    def summed(value):
        return (value[:, lanes_of(0)] + value[:, lanes_of(1)]) + (value[:, lanes_of(2)] + value[:, lanes_of(3)])

    for n in range(steps):
        fill_tables(seed, cos, sin, turn, n * step, (n + 1) * step)
        at = pl.ds(n * step, step)
        c_rows, s_rows = cos[at, :], sin[at, :]
        tc, ts = turn[0, at, :], turn[1, at, :]
        grad = columns(0)
        cg, sg = dot(c_rows, grad), dot(s_rows, grad)
        if n == 0:
            filt_copy.wait()
        re, im = filt[0, at, :], filt[1, at, :]
        for q in range(SPLIT):
            a, b = cg[:, lanes_of(q)], sg[:, lanes_of(q)]
            uv[0, at, lanes_of(q)] = (a * re + b * im).astype(BF16)
            uv[1, at, lanes_of(q)] = (b * re - a * im).astype(BF16)
        mixed = columns(1)
        cm, sm = dot(c_rows, mixed), dot(s_rows, mixed)
        sum_re = summed(cg * cm + sg * sm)
        sum_im = summed(sg * cm - cg * sm) * sign
        prod[0, at, :] = (sum_re * tc + sum_im * ts).astype(BF16)
        prod[1, at, :] = (sum_re * ts - sum_im * tc).astype(BF16)

    lags = dot_tn(prod[0], cos[...]) + dot_tn(prod[1], sin[...])
    row = lax.broadcasted_iota(jnp.int32, (LANES // 2, LANES), 0)
    col = lax.broadcasted_iota(jnp.int32, (LANES // 2, LANES), 1)
    row = jnp.where(odd == 0, row, LANES // 2 - 1 - row)
    fold = jnp.where((col == row) | (col == LANES - 1 - row), 1.0, 0.0).astype(BF16)
    upper = lags.astype(BF16)
    total = dot(fold, upper) + dot(fold, (lags - upper.astype(F32)).astype(BF16))
    for block in range(SEQ // BLOCK):
        home = place_ref[2 + block]
        folded[((z ^ home) & 1) * 4 + (home & 2) + (home >> 2)] = total[:, lanes_of(block)]
    keep[...] = folded[:4]
    give[...] = folded[4:].astype(BF16)


def back_kernel(uv, cos, sin, conv_hbm, conv, sem_out):
    step = 256
    steps = SEQ // step
    leaving = []
    size = SPLIT * (step // BLOCK)
    for n in range(steps):
        at = pl.ds(n * step, step)
        value = dot(cos[at, :], uv[0]) + dot(sin[at, :], uv[1])
        value = (value * (1.0 / SEQ)).astype(BF16)
        for i in range(step // BLOCK):
            for q in range(SPLIT):
                conv[n * size + SPLIT * i + q] = value[i * BLOCK:(i + 1) * BLOCK, lanes_of(q)]
        part = pl.ds(n * size, size)
        copy = pltpu.make_async_copy(conv.at[part], conv_hbm.at[part], sem_out.at[n])
        copy.start()
        leaving.append(copy)
    for copy in leaving:
        copy.wait()


def core(place, x, filt, seed):
    table = pltpu.VMEM((SEQ, SEQ), BF16)
    return pl.pallas_call(
        core_kernel,
        in_specs=[SMEM, VMEM, HBM, VMEM],
        out_specs=(VMEM,) * 5,
        out_shape=(
            jax.ShapeDtypeStruct((4, LANES // 2, BLOCK), F32),
            jax.ShapeDtypeStruct((4, LANES // 2, BLOCK), BF16),
            pltpu.VMEM((2, SEQ, WIDTH), BF16),
            table,
            table,
        ),
        scratch_shapes=[
            pltpu.VMEM((2, SEQ, LANES), F32),
            pltpu.VMEM((2, SEQ, LANES), F32),
            pltpu.VMEM((2, SEQ, LANES), BF16),
            pltpu.VMEM((8, LANES // 2, BLOCK), F32),
            pltpu.SemaphoreType.DMA((1,)),
        ],
        compiler_params=SMALL,
        cost_estimate=pl.CostEstimate(flops=5000 * MIB, bytes_accessed=4 * MIB, transcendentals=0),
        name="core",
    )(place, x, pltpu.with_memory_space_constraint(filt, pltpu.HBM), seed)


def back(uv, cos, sin):
    return pl.pallas_call(
        back_kernel,
        in_specs=[VMEM] * 3,
        out_specs=HBM,
        out_shape=pltpu.HBM((GROUPS, BLOCK, LANES), BF16),
        scratch_shapes=[pltpu.VMEM((GROUPS, BLOCK, LANES), BF16), pltpu.SemaphoreType.DMA((4,))],
        compiler_params=SMALL,
        cost_estimate=pl.CostEstimate(flops=2100 * MIB, bytes_accessed=MIB, transcendentals=0),
        name="back",
    )(uv, cos, sin)


def unpack_kernel(conv, k_in, v_in, lags, key_hbm, value_hbm, lags_hbm, key, value, sem_out, sem_lags):
    tiles = GROUPS // 2 // CUTS
    width = tiles * LANES
    lags_copy = pltpu.make_async_copy(lags, lags_hbm, sem_lags.at[0])
    lags_copy.start()
    low = lax.broadcasted_iota(jnp.int32, (BLOCK, LANES), 1) < LANES // 2
    leaving = []
    for j in range(CUTS):
        for t in range(j * tiles, (j + 1) * tiles):
            even = conv[2 * t].astype(F32)
            odd = conv[2 * t + 1].astype(F32)
            ahead, behind = jnp.where(low, even, odd), jnp.where(low, odd, even)
            for cols, grad in ((lanes_of(t), ahead), (lanes_of(GROUPS - 1 - t), behind)):
                key[:, cols] = (grad * v_in[:, cols].astype(F32)).astype(BF16)
                value[:, cols] = (grad * k_in[:, cols].astype(F32)).astype(BF16)
        for s, at in enumerate((j, 2 * CUTS - 1 - j)):
            cols = pl.ds(at * width, width)
            for m, (src, dst) in enumerate(((key, key_hbm), (value, value_hbm))):
                copy = pltpu.make_async_copy(src.at[:, cols], dst.at[:, cols], sem_out.at[j, s, m])
                copy.start()
                leaving.append(copy)
    lags_copy.wait()
    for copy in leaving:
        copy.wait()


def unpack(conv, k, v, lags):
    shape = jax.ShapeDtypeStruct(k.shape, BF16)
    whole = pltpu.VMEM(k.shape, BF16)
    return pl.pallas_call(
        unpack_kernel,
        in_specs=[VMEM] * 4,
        out_specs=(ANY,) * 3,
        out_shape=(shape, shape, jax.ShapeDtypeStruct(lags.shape, F32)),
        scratch_shapes=[whole, whole, pltpu.SemaphoreType.DMA((CUTS, 2, 2)), pltpu.SemaphoreType.DMA((1,))],
        compiler_params=SMALL,
        cost_estimate=pl.CostEstimate(flops=2 * MIB, bytes_accessed=5 * MIB, transcendentals=0),
        name="unpack",
    )(conv, k, v, lags)


def times_kernel(a, b, out):
    out[...] = (a[...].astype(F32) * b[...].astype(F32)).astype(BF16)


def times(a, b):
    block = pl.BlockSpec((BLOCK // 2, a.shape[1]), lambda i: (i, 0))
    return pl.pallas_call(
        times_kernel,
        grid=(2,),
        in_specs=[block, block],
        out_specs=block,
        out_shape=jax.ShapeDtypeStruct(a.shape, BF16),
        compiler_params=SMALL,
        cost_estimate=pl.CostEstimate(flops=1, bytes_accessed=1, transcendentals=0),
        name="times",
    )(a, b)


def swap_z(block, bit):
    return lax.ppermute(block, "z", [(i, i ^ (1 << bit)) for i in range(8)])


def sent_out(filters):
    homes = lag_homes()
    route = [(8 * l + n, 8 * n + homes[n][l]) for l in range(8) for n in range(8)]
    return lax.ppermute(filters, CTX_Z, route)[None]


def gathered_over_z(near):
    near = jnp.concatenate([near, swap_z(near, 2)], axis=0)
    near = jnp.concatenate([near, swap_z(near, 1)], axis=0)
    return near, swap_z(near, 0)


def halves(lags, bit):
    low, high = jnp.split(lags, 2, axis=0)
    first = (lax.axis_index("z") >> bit) % 2 == 0
    kept = lax.optimization_barrier(jnp.where(first, low, high))
    given = lax.optimization_barrier(jnp.where(first, high, low))
    return kept, given.astype(BF16)


def joined(kept, given, bit):
    other = lax.optimization_barrier(swap_z(given, bit).astype(F32))
    total = lax.optimization_barrier(kept + other)
    for halvings in (3, 2):
        total = lax.optimization_barrier(total * 0.5**halvings)
    return total


def sent_home(lags):
    homes = lag_homes()
    route = [(8 * n + homes[n][l], 8 * l + n) for l in range(8) for n in range(8)]
    return lax.ppermute(lags, CTX_Z, route)


def local(query_gate, key_gate, value_in, conv_out, out_grad, filters):
    home = jnp.asarray(lag_homes(), jnp.int32)[lax.axis_index(CTX)]
    place = jnp.concatenate([jnp.stack([lax.axis_index("core"), lax.axis_index("z")]).astype(jnp.int32), home])
    q, k, v, g = query_gate[0], key_gate[0], value_in[0], out_grad[0]
    x, near = lax.optimization_barrier((pack(q, g, k, v), sent_out(filters)))
    x = lax.all_to_all(x, PLANE, split_axis=0, concat_axis=0, tiled=True)

    near, far = gathered_over_z(near)
    filt, seed = filter_spectrum(place, near, far)
    filt, seed, query_grad = lax.optimization_barrier((filt, seed, times(g, conv_out[0])[None]))

    keep, give, uv, cos, sin = core(place, x, filt, seed)
    kept, given = halves(keep + swap_z(give, 0).astype(F32), 1)
    conv, kept, given = lax.optimization_barrier((back(uv, cos, sin), kept, given))
    conv = lax.all_to_all(conv, PLANE, split_axis=0, concat_axis=0, tiled=True)
    kept, given = halves(joined(kept, given, 1), 2)
    lags = joined(kept, given, 2)[0]
    key_grad, value_grad, filter_grad = unpack(conv, k, v, sent_home(lags))
    return query_grad, key_grad[None], value_grad[None], filter_grad


def solution(mesh):
    fine = Mesh(mesh.devices.reshape(2, 4, 8, 2, 2), ("xh", "y", "z", "xl", "core"))
    wide = P(("z", "xl", "core"), CTX, None)
    narrow = P(("z", "xl", "core"), CTX)
    return jax.shard_map(
        local,
        mesh=fine,
        in_specs=(wide,) * 5 + (narrow,),
        out_specs=(wide, wide, wide, narrow),
        check_vma=False,
    )
```

```python
import jax
import jax.numpy as jnp
import numpy as np
from jax import lax
from jax.experimental import pallas as pl
from jax.experimental.pallas import tpu as pltpu
from jax.sharding import Mesh
from jax.sharding import PartitionSpec as P

CTX = ("xh", "y")
PLANE = ("y", "core", "xh", "xl")
CTX_Z = ("xh", "y", "z")
SEQ = 1024
BLOCK = 128
LANES = 128
SPLIT = 4
WIDTH = SPLIT * LANES
GROUPS = 32
STEP = 32
CUTS = 4
MIB = 1024 * 1024
F32 = jnp.float32
BF16 = jnp.bfloat16


def ring(a, b, size):
    return min((a - b) % size, (b - a) % size)


def lag_homes():
    homes = []
    for n in range(8):
        far = sorted(range(8), key=lambda l: -(2 * (l // 4 != n // 4) + ring(l % 4, n % 4, 4)))
        near = sorted(range(8), key=lambda z: ring(z, n, 8))
        homes.append([near[far.index(l)] for l in range(8)])
    return homes


def slot_of(z, home):
    n = z ^ home
    return (n & 1) * 4 + (n & 2) + (n >> 2)


def chunk_at(n, r):
    return 8 * (n % 4) + 4 * (r % 2) + 2 * (n // 4) + r // 2


def dot(a, b):
    return jnp.dot(a, b, preferred_element_type=F32)


def dot_nt(a, b):
    return lax.dot_general(a, b, (((1,), (1,)), ((), ())), preferred_element_type=F32)


def dot_tn(a, b):
    return lax.dot_general(a, b, (((0,), (0,)), ((), ())), preferred_element_type=F32)


def seeds():
    odd = 2 * np.arange(SEQ, dtype=np.int64) + 1
    coarse = 2 * STEP * np.arange(SEQ // STEP, dtype=np.int64)
    fine = 2 * np.arange(STEP, dtype=np.int64) + 1
    out = []
    for part in (coarse, fine):
        angle = (np.multiply.outer(part, odd) % (8 * SEQ)).astype(np.float64) * (np.pi / (4 * SEQ))
        out += [np.cos(angle), np.sin(angle)]
    return np.stack(out).astype(np.float32)


def fill_tables(seed, cos, sin, turn, first, last):
    for a in range(first // STEP, last // STEP):
        ca, sa = seed[0, a:a + 1, :], seed[1, a:a + 1, :]
        c = ca * seed[2] - sa * seed[3]
        s = sa * seed[2] + ca * seed[3]
        rows = pl.ds(a * STEP, STEP)
        cos[rows, :] = c.astype(BF16)
        sin[rows, :] = s.astype(BF16)
        turn[0, rows, :] = jnp.broadcast_to(c[:, :1], (STEP, LANES))
        turn[1, rows, :] = jnp.broadcast_to(s[:, :1], (STEP, LANES))


def lanes_of(tile):
    return slice(tile * LANES, (tile + 1) * LANES)


def pack_kernel(q_hbm, g_hbm, k_hbm, v_hbm, x_hbm, buf, out, sem_in, sem_out):
    tiles = GROUPS // 2 // CUTS
    width = tiles * LANES
    low = lax.broadcasted_iota(jnp.int32, (BLOCK, LANES), 1) < LANES // 2
    arriving = []
    for j in range(CUTS):
        copies = []
        for i, ref in enumerate((q_hbm, g_hbm, k_hbm, v_hbm)):
            for s, at in enumerate((j, 2 * CUTS - 1 - j)):
                cols = pl.ds(at * width, width)
                copies.append(pltpu.make_async_copy(ref.at[:, cols], buf.at[i, :, cols], sem_in.at[j, i, s]))
        for copy in copies:
            copy.start()
        arriving.append(copies)
    leaving = []
    for j in range(CUTS):
        for copy in arriving[j]:
            copy.wait()
        for t in range(j * tiles, (j + 1) * tiles):
            ahead, behind = lanes_of(t), lanes_of(GROUPS - 1 - t)
            even, odd = (chunk_at(block // 4, block % 4) for block in (2 * t, 2 * t + 1))
            for kind in range(2):
                a, b = 2 * kind, 2 * kind + 1
                f = buf[a, :, ahead].astype(F32) * buf[b, :, ahead].astype(F32)
                r = buf[a, :, behind].astype(F32) * buf[b, :, behind].astype(F32)
                out[even, kind] = jnp.where(low, f, r).astype(BF16)
                out[odd, kind] = jnp.where(low, r, f).astype(BF16)
            for chunk in (even, odd):
                copy = pltpu.make_async_copy(out.at[chunk], x_hbm.at[chunk], sem_out.at[chunk])
                copy.start()
                leaving.append(copy)
    for copy in leaving:
        copy.wait()


ANY = pl.BlockSpec(memory_space=pl.ANY)
VMEM = pl.BlockSpec(memory_space=pltpu.VMEM)
SMEM = pl.BlockSpec(memory_space=pltpu.SMEM)
HBM = pl.BlockSpec(memory_space=pltpu.HBM)
LIMIT = pltpu.CompilerParams(vmem_limit_bytes=60 * MIB)
SMALL = pltpu.CompilerParams(vmem_limit_bytes=24 * MIB)


def pack(q, g, k, v):
    return pl.pallas_call(
        pack_kernel,
        in_specs=[ANY] * 4,
        out_specs=ANY,
        out_shape=jax.ShapeDtypeStruct((GROUPS, 2, BLOCK, LANES), BF16),
        scratch_shapes=[
            pltpu.VMEM((4,) + q.shape, BF16),
            pltpu.VMEM((GROUPS, 2, BLOCK, LANES), BF16),
            pltpu.SemaphoreType.DMA((CUTS, 4, 2)),
            pltpu.SemaphoreType.DMA((GROUPS,)),
        ],
        compiler_params=LIMIT,
        cost_estimate=pl.CostEstimate(flops=2 * MIB, bytes_accessed=6 * MIB, transcendentals=0),
        name="pack",
    )(q, g, k, v)


def filter_kernel(place_ref, seed, near, far, filt_hbm, seed_out, filt, rows_in, cos, sin, turn, sem):
    odd, z = place_ref[0], place_ref[1]
    step = 256
    row = lax.broadcasted_iota(jnp.int32, (LANES, LANES // 2), 0)
    col = lax.broadcasted_iota(jnp.int32, (LANES, LANES // 2), 1)
    ahead = row - jnp.where(odd == 0, 0, LANES // 2)
    behind = jnp.where(odd == 0, LANES, LANES // 2) - 1 - row
    spread = jnp.where((col == ahead) | (col == behind), 1.0, 0.0).astype(BF16)
    for block in range(SEQ // BLOCK):
        slot = slot_of(z, place_ref[2 + block])
        lags = jnp.where(slot < 4, near[slot % 4], far[slot % 4]).astype(BF16)
        rows_in[:, lanes_of(block)] = dot(spread, lags).astype(BF16)
    sign = strand_sign(odd)
    for n in range(SEQ // step):
        fill_tables(seed, cos, sin, turn, n * step, (n + 1) * step)
        at = pl.ds(n * step, step)
        fc, fs = dot_nt(cos[at, :], rows_in[...]), dot_nt(sin[at, :], rows_in[...])
        tc, ts = turn[0, at, :], turn[1, at, :]
        filt[0, at, :] = fc * tc + fs * ts
        filt[1, at, :] = (fc * ts - fs * tc) * sign
    copy = pltpu.make_async_copy(filt, filt_hbm, sem.at[0])
    copy.start()
    seed_out[...] = seed[...]
    copy.wait()


def filter_spectrum(place, near, far):
    seed = jnp.asarray(seeds())
    return pl.pallas_call(
        filter_kernel,
        in_specs=[SMEM, VMEM, VMEM, VMEM],
        out_specs=(HBM, VMEM),
        out_shape=(pltpu.HBM((2, SEQ, LANES), F32), jax.ShapeDtypeStruct(seed.shape, F32)),
        scratch_shapes=[
            pltpu.VMEM((2, SEQ, LANES), F32),
            pltpu.VMEM((LANES, SEQ), BF16),
            pltpu.VMEM((SEQ, SEQ), BF16),
            pltpu.VMEM((SEQ, SEQ), BF16),
            pltpu.VMEM((2, SEQ, LANES), F32),
            pltpu.SemaphoreType.DMA((1,)),
        ],
        compiler_params=SMALL,
        cost_estimate=pl.CostEstimate(flops=1, bytes_accessed=1, transcendentals=0),
        name="filter_spectrum",
    )(place, seed, near, far)


def strand_sign(odd):
    lane = lax.broadcasted_iota(jnp.int32, (1, LANES), 1)
    return jnp.where((lane < LANES // 2) == (odd == 0), -1.0, 1.0).astype(F32)


def core_kernel(place_ref, x, filt_hbm, seed, keep, give, uv, cos, sin, filt, turn, prod, folded, sem_in):
    odd, z = place_ref[0], place_ref[1]
    step = 256
    steps = SEQ // step
    sign = strand_sign(odd)
    filt_copy = pltpu.make_async_copy(filt_hbm, filt, sem_in.at[0])
    filt_copy.start()
    def columns(kind):
        tiles = [[x[chunk_at(i, q), kind] for i in range(SEQ // BLOCK)] for q in range(SPLIT)]
        return jnp.concatenate([jnp.concatenate(tile, axis=0) for tile in tiles], axis=1)

    def summed(value):
        return (value[:, lanes_of(0)] + value[:, lanes_of(1)]) + (value[:, lanes_of(2)] + value[:, lanes_of(3)])

    for n in range(steps):
        fill_tables(seed, cos, sin, turn, n * step, (n + 1) * step)
        at = pl.ds(n * step, step)
        c_rows, s_rows = cos[at, :], sin[at, :]
        tc, ts = turn[0, at, :], turn[1, at, :]
        grad = columns(0)
        cg, sg = dot(c_rows, grad), dot(s_rows, grad)
        if n == 0:
            filt_copy.wait()
        re, im = filt[0, at, :], filt[1, at, :]
        for q in range(SPLIT):
            a, b = cg[:, lanes_of(q)], sg[:, lanes_of(q)]
            uv[0, at, lanes_of(q)] = (a * re + b * im).astype(BF16)
            uv[1, at, lanes_of(q)] = (b * re - a * im).astype(BF16)
        mixed = columns(1)
        cm, sm = dot(c_rows, mixed), dot(s_rows, mixed)
        sum_re = summed(cg * cm + sg * sm)
        sum_im = summed(sg * cm - cg * sm) * sign
        prod[0, at, :] = (sum_re * tc + sum_im * ts).astype(BF16)
        prod[1, at, :] = (sum_re * ts - sum_im * tc).astype(BF16)

    lags = dot_tn(prod[0], cos[...]) + dot_tn(prod[1], sin[...])
    row = lax.broadcasted_iota(jnp.int32, (LANES // 2, LANES), 0)
    col = lax.broadcasted_iota(jnp.int32, (LANES // 2, LANES), 1)
    row = jnp.where(odd == 0, row, LANES // 2 - 1 - row)
    fold = jnp.where((col == row) | (col == LANES - 1 - row), 1.0, 0.0).astype(BF16)
    upper = lags.astype(BF16)
    total = dot(fold, upper) + dot(fold, (lags - upper.astype(F32)).astype(BF16))
    for block in range(SEQ // BLOCK):
        home = place_ref[2 + block]
        folded[((z ^ home) & 1) * 4 + (home & 2) + (home >> 2)] = total[:, lanes_of(block)]
    keep[...] = folded[:4]
    give[...] = folded[4:].astype(BF16)


def back_kernel(uv, cos, sin, conv_hbm, conv, sem_out):
    step = 256
    steps = SEQ // step
    leaving = []
    for n in range(steps):
        at = pl.ds(n * step, step)
        value = dot(cos[at, :], uv[0]) + dot(sin[at, :], uv[1])
        value = (value * (1.0 / SEQ)).astype(BF16)
        for i in range(step // BLOCK):
            for q in range(SPLIT):
                chunk = chunk_at(n * (step // BLOCK) + i, q)
                conv[chunk] = value[i * BLOCK:(i + 1) * BLOCK, lanes_of(q)]
                copy = pltpu.make_async_copy(conv.at[chunk], conv_hbm.at[chunk], sem_out.at[chunk])
                copy.start()
                leaving.append(copy)
    for copy in leaving:
        copy.wait()


def core(place, x, filt, seed):
    table = pltpu.VMEM((SEQ, SEQ), BF16)
    return pl.pallas_call(
        core_kernel,
        in_specs=[SMEM, VMEM, HBM, VMEM],
        out_specs=(VMEM,) * 5,
        out_shape=(
            jax.ShapeDtypeStruct((4, LANES // 2, BLOCK), F32),
            jax.ShapeDtypeStruct((4, LANES // 2, BLOCK), BF16),
            pltpu.VMEM((2, SEQ, WIDTH), BF16),
            table,
            table,
        ),
        scratch_shapes=[
            pltpu.VMEM((2, SEQ, LANES), F32),
            pltpu.VMEM((2, SEQ, LANES), F32),
            pltpu.VMEM((2, SEQ, LANES), BF16),
            pltpu.VMEM((8, LANES // 2, BLOCK), F32),
            pltpu.SemaphoreType.DMA((1,)),
        ],
        compiler_params=SMALL,
        cost_estimate=pl.CostEstimate(flops=5000 * MIB, bytes_accessed=4 * MIB, transcendentals=0),
        name="core",
    )(place, x, pltpu.with_memory_space_constraint(filt, pltpu.HBM), seed)


def back(uv, cos, sin):
    return pl.pallas_call(
        back_kernel,
        in_specs=[VMEM] * 3,
        out_specs=HBM,
        out_shape=pltpu.HBM((GROUPS, BLOCK, LANES), BF16),
        scratch_shapes=[pltpu.VMEM((GROUPS, BLOCK, LANES), BF16), pltpu.SemaphoreType.DMA((GROUPS,))],
        compiler_params=SMALL,
        cost_estimate=pl.CostEstimate(flops=2100 * MIB, bytes_accessed=MIB, transcendentals=0),
        name="back",
    )(uv, cos, sin)


def unpack_kernel(conv, k_in, v_in, lags, key_hbm, value_hbm, lags_hbm, key, value, sem_out, sem_lags):
    tiles = GROUPS // 2 // CUTS
    width = tiles * LANES
    lags_copy = pltpu.make_async_copy(lags, lags_hbm, sem_lags.at[0])
    lags_copy.start()
    low = lax.broadcasted_iota(jnp.int32, (BLOCK, LANES), 1) < LANES // 2
    leaving = []
    for j in range(CUTS):
        for t in range(j * tiles, (j + 1) * tiles):
            even = conv[chunk_at(t // 2, 2 * t % 4)].astype(F32)
            odd = conv[chunk_at(t // 2, 2 * t % 4 + 1)].astype(F32)
            ahead, behind = jnp.where(low, even, odd), jnp.where(low, odd, even)
            for cols, grad in ((lanes_of(t), ahead), (lanes_of(GROUPS - 1 - t), behind)):
                key[:, cols] = (grad * v_in[:, cols].astype(F32)).astype(BF16)
                value[:, cols] = (grad * k_in[:, cols].astype(F32)).astype(BF16)
        for s, at in enumerate((j, 2 * CUTS - 1 - j)):
            cols = pl.ds(at * width, width)
            for m, (src, dst) in enumerate(((key, key_hbm), (value, value_hbm))):
                copy = pltpu.make_async_copy(src.at[:, cols], dst.at[:, cols], sem_out.at[j, s, m])
                copy.start()
                leaving.append(copy)
    lags_copy.wait()
    for copy in leaving:
        copy.wait()


def unpack(conv, k, v, lags):
    shape = jax.ShapeDtypeStruct(k.shape, BF16)
    whole = pltpu.VMEM(k.shape, BF16)
    return pl.pallas_call(
        unpack_kernel,
        in_specs=[VMEM] * 4,
        out_specs=(ANY,) * 3,
        out_shape=(shape, shape, jax.ShapeDtypeStruct(lags.shape, F32)),
        scratch_shapes=[whole, whole, pltpu.SemaphoreType.DMA((CUTS, 2, 2)), pltpu.SemaphoreType.DMA((1,))],
        compiler_params=SMALL,
        cost_estimate=pl.CostEstimate(flops=2 * MIB, bytes_accessed=5 * MIB, transcendentals=0),
        name="unpack",
    )(conv, k, v, lags)


def times_kernel(a, b, out):
    out[...] = (a[...].astype(F32) * b[...].astype(F32)).astype(BF16)


def times(a, b):
    block = pl.BlockSpec((BLOCK // 2, a.shape[1]), lambda i: (i, 0))
    return pl.pallas_call(
        times_kernel,
        grid=(2,),
        in_specs=[block, block],
        out_specs=block,
        out_shape=jax.ShapeDtypeStruct(a.shape, BF16),
        compiler_params=SMALL,
        cost_estimate=pl.CostEstimate(flops=1, bytes_accessed=1, transcendentals=0),
        name="times",
    )(a, b)


def swap_z(block, bit):
    return lax.ppermute(block, "z", [(i, i ^ (1 << bit)) for i in range(8)])


def sent_out(filters):
    homes = lag_homes()
    route = [(8 * l + n, 8 * n + homes[n][l]) for l in range(8) for n in range(8)]
    return lax.ppermute(filters, CTX_Z, route)[None]


def gathered_over_z(near):
    near = jnp.concatenate([near, swap_z(near, 2)], axis=0)
    near = jnp.concatenate([near, swap_z(near, 1)], axis=0)
    return near, swap_z(near, 0)


def halves(lags, bit):
    low, high = jnp.split(lags, 2, axis=0)
    first = (lax.axis_index("z") >> bit) % 2 == 0
    kept = lax.optimization_barrier(jnp.where(first, low, high))
    given = lax.optimization_barrier(jnp.where(first, high, low))
    return kept, given.astype(BF16)


def joined(kept, given, bit):
    other = lax.optimization_barrier(swap_z(given, bit).astype(F32))
    total = lax.optimization_barrier(kept + other)
    for halvings in (3, 2):
        total = lax.optimization_barrier(total * 0.5**halvings)
    return total


def sent_home(lags):
    homes = lag_homes()
    route = [(8 * n + homes[n][l], 8 * l + n) for l in range(8) for n in range(8)]
    return lax.ppermute(lags, CTX_Z, route)


def local(query_gate, key_gate, value_in, conv_out, out_grad, filters):
    home = jnp.asarray(lag_homes(), jnp.int32)[lax.axis_index(CTX)]
    place = jnp.concatenate([jnp.stack([lax.axis_index("core"), lax.axis_index("z")]).astype(jnp.int32), home])
    q, k, v, g = query_gate[0], key_gate[0], value_in[0], out_grad[0]
    x, near = lax.optimization_barrier((pack(q, g, k, v), sent_out(filters)))
    x = lax.all_to_all(x, PLANE, split_axis=0, concat_axis=0, tiled=True)

    near, far = gathered_over_z(near)
    filt, seed = filter_spectrum(place, near, far)
    filt, seed, query_grad = lax.optimization_barrier((filt, seed, times(g, conv_out[0])[None]))

    keep, give, uv, cos, sin = core(place, x, filt, seed)
    kept, given = halves(keep + swap_z(give, 0).astype(F32), 1)
    conv, kept, given = lax.optimization_barrier((back(uv, cos, sin), kept, given))
    conv = lax.all_to_all(conv, PLANE, split_axis=0, concat_axis=0, tiled=True)
    kept, given = halves(joined(kept, given, 1), 2)
    lags = joined(kept, given, 2)[0]
    key_grad, value_grad, filter_grad = unpack(conv, k, v, sent_home(lags))
    return query_grad, key_grad[None], value_grad[None], filter_grad


def solution(mesh):
    fine = Mesh(mesh.devices.reshape(2, 4, 8, 2, 2), ("xh", "y", "z", "xl", "core"))
    wide = P(("z", "xl", "core"), CTX, None)
    narrow = P(("z", "xl", "core"), CTX)
    return jax.shard_map(
        local,
        mesh=fine,
        in_specs=(wide,) * 5 + (narrow,),
        out_specs=(wide, wide, wide, narrow),
        check_vma=False,
    )
```
